512 devices in a mesh: enc: 32 (over x, y, core), seq: 16 (over z).
Axes of the slice: x: 4, y: 4, z: 16, core: 2. Of those that a mesh axis runs over, the one named last changes fastest.
Arguments:
- tile_maps: bfloat16 [32, 256, 8, 8, 512], P('enc', 'seq'), may hold values from -6 to 6
- conv_weight: bfloat16 [4608, 512], P('enc'), may hold values from -0.15625 to 0.15625
- norm_gain: float32 [512], replicated, may hold values from 0.5 to 1.5
- norm_bias: float32 [512], replicated, may hold values from -3 to 3
- tile_proj: bfloat16 [512, 768], replicated, may hold values from -1 to 1
- positions: int32 [32, 256], P('enc'), may hold values from 0 to 4095, as said below
- slide_cache: bfloat16 [32, 4096, 768], P('enc', 'seq'), may hold values from -16 to 16
- project_in: bfloat16 [768, 2304], P(None, 'seq'), may hold values from -0.4375 to 0.4375
- project_out: bfloat16 [768, 768], replicated, may hold values from -0.21875 to 0.21875
- head_rates: int32 [16], replicated, may hold values from 1 to 8, as said below
Outputs:
- attended: bfloat16 [32, 4096, 768], P('enc', 'seq')
The draws below stay inside these ranges and needn't reach their ends.
Inputs may be any that keep to these rules, and one draw needn't show every extreme that they name: Positions of one slide are distinct. Of the 16 tiles of one device (entries d * 16 to (d + 1) * 16 - 1), at most 2 lie in one block of 256 positions; in every slide one block receives exactly 2 from every device. `head_rates`: each of 1, 2, 4 and 8 is the rate of 4 heads.
All inputs are finite; a program needn't handle non-finite values.
Results may differ from the reference program's by a relative error of at most 0.017.
Values may be sent and summed in bfloat16 or wider, within the bound.
No kernel may reach another device: no remote copies, remote signals or barrier semaphores. Data moves between devices by JAX's collectives and lax.ppermute only.
A program may use at most 64 MiB of HBM per device.

```python
from functools import partial
import jax
import jax.numpy as jnp
from jax import lax

C = 512
SIDE = 8
E = 768
HEADS = 16
NEW_DEV = 16
LOC = 256
CAP = 2
SLIDES = 32
NEWS = 256
L = 4096
N_SEQ = 16


def slide_positions(key):
    key_source, key_full, key_layout = jax.random.split(key, 3)
    slot_count = N_SEQ * CAP
    full_block = jax.random.randint(key_full, (), 0, N_SEQ)
    owner_of_slot = jnp.arange(slot_count) // CAP

    def one_source(source_key):
        key_order, key_shuffle = jax.random.split(source_key)
        ranking = jax.random.permutation(key_order, slot_count)
        score = ranking - slot_count * (owner_of_slot == full_block).astype(jnp.int32)
        chosen = jnp.argsort(score, stable=True)[:NEW_DEV]
        return jax.random.permutation(key_shuffle, chosen)
    chosen = jax.vmap(one_source)(jax.random.split(key_source, N_SEQ))

    def one_layout(layout_key):
        return jax.random.permutation(layout_key, LOC)
    layout = jax.vmap(one_layout)(jax.random.split(key_layout, N_SEQ))
    owners = chosen // CAP
    column = jnp.arange(N_SEQ)[:, None] * CAP + chosen % CAP
    offset = layout[owners, column]
    return (owners * LOC + offset).reshape(N_SEQ * NEW_DEV).astype(jnp.int32)


def draw_positions(key, part):
    return jax.vmap(slide_positions)(jax.random.split(key, SLIDES)).astype(jnp.int32)


def draw_slide_cache(key, part):
    key_base = jax.random.fold_in(key, 0)
    full_shape = (SLIDES, L, E)
    return jnp.clip(jax.random.normal(key_base, full_shape, jnp.float32), -6.0, 6.0).astype(jnp.bfloat16)


def draw_head_rates(key, part):
    shuffled = jax.random.permutation(key, HEADS)
    return jnp.left_shift(jnp.int32(1), (shuffled % 4).astype(jnp.int32)).astype(jnp.int32)


def spiked(drawn, rng, source, target, blocks, factor):
    def block_of(dim):
        return (jnp.arange(drawn.shape[dim]) // (drawn.shape[dim] // blocks)).reshape((-1,) + (1,) * (drawn.ndim - 1 - dim))

    near = jax.random.permutation(rng, blocks)[block_of(target)]
    second = (block_of(target) + blocks // 2) % blocks
    return jnp.where((block_of(source) == near) | (block_of(source) == second), factor * drawn, drawn)


def level_of(key, extent, cuts, least, top_value):
    loudness = 1.0
    for position, parts in cuts:
        steps = jax.random.uniform(jax.random.fold_in(jax.random.fold_in(key, 6), position), (parts,), jnp.float32, least / len(cuts), top_value / len(cuts))
        loudness = loudness * jnp.repeat(jnp.exp(steps), extent[position] // parts).reshape((-1,) + (1,) * (len(extent) - 1 - position))
    return loudness


def bell_draw(own_key, shape, spread, limit, shards=(), held_as=jnp.bfloat16):
    array = spread * jax.random.normal(own_key, shape, jnp.float32)
    if shards:
        array = array * level_of(own_key, shape, shards, -0.22, 0.18)
    return jnp.clip(array, -limit, limit).astype(held_as)


def bell_draw_with(stream_key, extent, scale, reach, pieces, heavy, kind=jnp.bfloat16):
    values = scale * jax.random.normal(stream_key, extent, jnp.float32)
    if pieces:
        values = values * level_of(stream_key, extent, pieces, -0.22, 0.18)
    return jnp.clip(spiked(values, jax.random.fold_in(stream_key, 3), *heavy), -reach, reach).astype(kind)


def setup_inputs(seed: int = 0) -> dict:
    seeds = jax.random.split(jax.random.key(seed), 11)
    tile_maps = bell_draw(seeds[0], (SLIDES, NEWS, SIDE, SIDE, C), 1.0, 6.0, ((0, 32), (1, 16)))
    conv_weight = bell_draw_with(seeds[1], (9 * C, C), (9 * C) ** -0.5, 0.15625, ((0, 32),), (0, 1, 32, 2.75))
    norm_gain = jnp.clip(1.0 + 0.1 * jax.random.normal(seeds[2], (C,), jnp.float32), 0.5, 1.5)
    norm_bias = bell_draw(seeds[3], (C,), 0.5, 3.0, (), jnp.float32)
    tile_proj = bell_draw(seeds[4], (C, E), (C // 16) ** -0.5, 1.0)
    positions = draw_positions(jax.random.fold_in(seeds[10], 71), 0)
    slide_cache = draw_slide_cache(jax.random.fold_in(seeds[10], 71), 0)
    project_in = bell_draw(seeds[7], (E, 3 * E), 192 ** -0.5, 0.4375, ((1, 16),))
    project_out = bell_draw(seeds[8], (E, E), E ** -0.5, 0.21875)
    head_rates = draw_head_rates(jax.random.fold_in(seeds[10], 71), 0)
    return {"tile_maps": tile_maps, "conv_weight": conv_weight, "norm_gain": norm_gain, "norm_bias": norm_bias, "tile_proj": tile_proj, "positions": positions, "slide_cache": slide_cache, "project_in": project_in, "project_out": project_out, "head_rates": head_rates}


def encode(tile_maps, conv_weight, norm_gain, norm_bias, tile_proj):
    tile_count, side_len, _, channels = tile_maps.shape
    padded = jnp.pad(tile_maps, ((0, 0), (1, 1), (1, 1), (0, 0)))
    columns = jnp.concatenate([padded[:, row_shift:row_shift + side_len, col_shift:col_shift + side_len, :] for row_shift in range(3) for col_shift in range(3)], axis=-1)
    columns = columns.reshape(tile_count * side_len * side_len, 9 * channels)
    convolved = jnp.dot(columns, conv_weight, preferred_element_type=jnp.float32)
    activated = jnp.maximum(convolved * norm_gain + norm_bias, 0.0) + tile_maps.reshape(-1, channels).astype(jnp.float32)
    pooled = jnp.mean(activated.reshape(tile_count, side_len * side_len, channels), axis=1).astype(jnp.bfloat16)
    return jnp.dot(pooled, tile_proj, preferred_element_type=jnp.float32).astype(jnp.bfloat16)


def dilated_head(query_rows, key_rows, value_rows, offset, dilation):
    length, head_feature_width = query_rows.shape
    block_len = length // 8
    offset = offset.astype(jnp.int32)

    def select(matrix):
        folded = matrix.reshape(length // dilation, dilation, head_feature_width)
        picked = lax.dynamic_slice_in_dim(folded, offset, 1, 1)
        return picked.reshape(length // dilation // block_len, block_len, head_feature_width).astype(jnp.float32)

    query_matrix = select(query_rows)
    selected_key_rows = select(key_rows)
    value_matrix = select(value_rows)
    score_matrix = jnp.einsum("fnp,fjp->fnj", query_matrix, selected_key_rows) * (head_feature_width ** -0.5)
    row_max = jnp.max(score_matrix, axis=-1, keepdims=True)
    raised = jnp.exp(score_matrix - row_max)
    attention_weight = (raised / jnp.sum(raised, axis=-1, keepdims=True)).astype(jnp.bfloat16)
    mixed_output = jnp.einsum("tln,tne->tle", attention_weight.astype(jnp.float32), value_matrix).astype(jnp.bfloat16)
    placed = jnp.zeros((length // dilation, dilation, head_feature_width), jnp.bfloat16)
    placed = lax.dynamic_update_slice_in_dim(placed, mixed_output.reshape(length // dilation, 1, head_feature_width), offset, 1)
    return placed.reshape(length, head_feature_width)


def reference(tile_maps, conv_weight, norm_gain, norm_bias, tile_proj, positions, slide_cache, project_in, project_out, head_rates):
    head_feature_width = E // HEADS
    branches = [partial(dilated_head, dilation=factor) for factor in (1, 2, 4, 8)]

    def one_slide(operands):
        slide_tiles, slide_list, cached = operands
        embedded = encode(slide_tiles, conv_weight, norm_gain, norm_bias, tile_proj)
        merged = cached.at[slide_list].set(embedded)
        projections = jnp.dot(merged, project_in, preferred_element_type=jnp.float32).astype(jnp.bfloat16)
        head_outputs = []
        for head_index in range(HEADS):
            dilation = head_rates[head_index]
            branch = ((dilation >= 2).astype(jnp.int32) + (dilation >= 4).astype(jnp.int32) + (dilation >= 8).astype(jnp.int32)).astype(jnp.int32)
            column_base = head_index * 3 * head_feature_width
            query_rows = projections[:, column_base:column_base + head_feature_width]
            key_rows = projections[:, column_base + head_feature_width:column_base + 2 * head_feature_width]
            value_rows = projections[:, column_base + 2 * head_feature_width:column_base + 3 * head_feature_width]
            offset = (jnp.int32(head_index) % dilation).astype(jnp.int32)
            head_outputs.append(lax.switch(branch, branches, query_rows, key_rows, value_rows, offset))
        head_out = jnp.concatenate(head_outputs, axis=1)
        return jnp.dot(head_out, project_out, preferred_element_type=jnp.float32).astype(jnp.bfloat16)

    return lax.map(one_slide, (tile_maps, positions, slide_cache))
```

```python
from functools import partial

import jax
import jax.numpy as jnp
from jax import lax
from jax.experimental import pallas as pl
from jax.experimental.pallas import tpu as pltpu
from jax.sharding import PartitionSpec as P

E = 768
HEADS = 16
WIDTH = E // HEADS
SEGMENT = 512
STEP_ROWS = 512


def attend(rate, offset, table, out_ref):
    length = table.shape[1]
    loc = out_ref.shape[2]
    spread = None
    if rate > 1:
        source = lax.broadcasted_iota(jnp.int32, (128, 128 * rate), 0)
        target = lax.broadcasted_iota(jnp.int32, (128, 128 * rate), 1)
        spread = (target == offset + rate * source).astype(jnp.float32).astype(jnp.bfloat16)
    lane = lax.broadcasted_iota(jnp.int32, (SEGMENT, 128), 1)

    def segment(index, carry):
        start = index * (SEGMENT * rate) + offset
        if rate == 1:
            start = pl.multiple_of(index * SEGMENT, SEGMENT)
            rows = pl.ds(start, SEGMENT)
        else:
            rows = pl.ds(start, SEGMENT, stride=rate)
        query_value = table[0, rows, :]
        keys = table[1, rows, :].astype(jnp.bfloat16)
        with_ones = jnp.where(lane == 112, 1.0, query_value).astype(jnp.bfloat16)
        query_value = query_value.astype(jnp.bfloat16)
        for part in range(SEGMENT // 256):
            queries = query_value[part * 256 : (part + 1) * 256]
            scores = lax.dot_general(
                keys, queries, (((1,), (1,)), ((), ())), preferred_element_type=jnp.float32
            )
            top = jnp.max(scores, axis=0, keepdims=True)
            raised = jnp.exp((scores - top) * WIDTH**-0.5).astype(jnp.bfloat16)
            mixed = lax.dot_general(
                with_ones, raised, (((0,), (0,)), ((), ())), preferred_element_type=jnp.float32
            )
            result = (mixed[64:112] / mixed[112:113]).astype(jnp.bfloat16)
            if rate == 1:
                out_ref[index * (SEGMENT // loc) + part] = result
            else:
                for half in range(2):
                    wide = jnp.dot(
                        result[:, half * 128 : (half + 1) * 128],
                        spread,
                        preferred_element_type=jnp.float32,
                    ).astype(jnp.bfloat16)
                    blocks = 128 * rate // loc
                    first = (index * 4 + part * 2 + half) * blocks
                    for block in range(blocks):
                        out_ref[first + block] = wide[:, block * loc : (block + 1) * loc]
        return carry

    lax.fori_loop(0, length // (SEGMENT * rate), segment, 0)


def head_kernel(places, choice, rows_ref, fresh_ref, weight_ref, out_ref, table, fresh):
    step = pl.program_id(0)
    made = jnp.dot(rows_ref[...], weight_ref[...], preferred_element_type=jnp.float32)
    made = made.astype(jnp.bfloat16).astype(jnp.float32)
    block = pl.ds(pl.multiple_of(step * STEP_ROWS, STEP_ROWS), STEP_ROWS)
    table[0, block, :] = made[:, :128]
    table[1, block, :] = made[:, 128:]

    @pl.when(step == pl.num_programs(0) - 1)
    def _():
        made_fresh = jnp.dot(fresh_ref[...], weight_ref[...], preferred_element_type=jnp.float32)
        made_fresh = made_fresh.astype(jnp.bfloat16).astype(jnp.float32)
        fresh[0] = made_fresh[:, :128]
        fresh[1] = made_fresh[:, 128:]

        def place(group, carry):
            for inner in range(8):
                tile = group * 8 + inner
                where = places[tile]
                for side in range(2):
                    table[side, pl.ds(where, 1), :] = fresh[side, pl.ds(tile, 1), :]
            return carry

        lax.fori_loop(0, fresh.shape[1] // 8, place, 0)
        for rate in (1, 2, 4, 8):
            pl.when(choice[0] == rate)(partial(attend, rate, choice[1], table, out_ref))


def head_attention(places, choice, rows, fresh, weight, seq_count):
    length = rows.shape[0]
    loc = length // seq_count
    return pl.pallas_call(
        head_kernel,
        out_shape=jax.ShapeDtypeStruct((seq_count, WIDTH, loc), jnp.bfloat16),
        grid_spec=pltpu.PrefetchScalarGridSpec(
            num_scalar_prefetch=2,
            grid=(length // STEP_ROWS,),
            in_specs=[
                pl.BlockSpec((STEP_ROWS, E), lambda i, *_: (i, 0)),
                pl.BlockSpec(fresh.shape, lambda i, *_: (0, 0)),
                pl.BlockSpec(weight.shape, lambda i, *_: (0, 0)),
            ],
            out_specs=pl.BlockSpec((seq_count, WIDTH, loc), lambda i, *_: (0, 0, 0)),
            scratch_shapes=[
                pltpu.VMEM((2, length, 128), jnp.float32),
                pltpu.VMEM((2, fresh.shape[0], 128), jnp.float32),
            ],
        ),
        compiler_params=pltpu.CompilerParams(
            dimension_semantics=("arbitrary",), vmem_limit_bytes=40 * 1024 * 1024
        ),
        cost_estimate=pl.CostEstimate(
            flops=2 * length * E * 256, bytes_accessed=rows.size * 2, transcendentals=length * SEGMENT
        ),
    )(places, choice, rows, fresh, weight)


def spread_to(shard, axis, count, groups=None):
    copies = jnp.broadcast_to(shard[None], (count,) + shard.shape)
    return lax.all_to_all(
        copies, axis, split_axis=0, concat_axis=0, tiled=True, axis_index_groups=groups
    )


def whole_weight(conv_weight):
    enc_count = lax.axis_size("enc")
    chips = enc_count // 2
    groups = [[2 * chip + core for chip in range(chips)] for core in range(2)]
    own = spread_to(conv_weight, "enc", chips, groups)
    other = lax.ppermute(own, "enc", [(e, e ^ 1) for e in range(enc_count)])
    first_core = lax.axis_index("enc") % 2 == 0
    even = jnp.where(first_core, own, other)
    odd = jnp.where(first_core, other, own)
    return jnp.stack([even, odd], axis=1).reshape(-1, conv_weight.shape[1])


def shards(
    tile_maps,
    conv_weight,
    norm_gain,
    norm_bias,
    tile_proj,
    positions,
    slide_cache,
    project_in,
    project_out,
    head_rates,
):
    tile_count = tile_maps.shape[1]
    side_len = tile_maps.shape[2]
    channels = tile_maps.shape[4]
    seq_count = lax.axis_size("seq")
    my_index = lax.axis_index("seq")

    with jax.named_scope("rows"):
        rows = lax.all_gather(slide_cache[0], "seq", axis=0, tiled=True)

    with jax.named_scope("encode"):
        images = tile_maps[0]
        padded = jnp.pad(images, ((0, 0), (1, 1), (1, 1), (0, 0)))
        columns = jnp.concatenate(
            [
                padded[:, row_shift : row_shift + side_len, col_shift : col_shift + side_len, :]
                for row_shift in range(3)
                for col_shift in range(3)
            ],
            axis=-1,
        )
        columns = columns.reshape(tile_count * side_len * side_len, 9 * channels)
        convolved = jnp.dot(columns, whole_weight(conv_weight), preferred_element_type=jnp.float32)
        activated = jnp.maximum(convolved * norm_gain + norm_bias, 0.0) + images.reshape(
            -1, channels
        ).astype(jnp.float32)
        pooled = jnp.mean(
            activated.reshape(tile_count, side_len * side_len, channels), axis=1
        ).astype(jnp.bfloat16)
        embedded = jnp.dot(pooled, tile_proj, preferred_element_type=jnp.float32).astype(
            jnp.bfloat16
        )

    with jax.named_scope("fresh"):
        fresh = spread_to(embedded, "seq", seq_count).reshape(-1, E)

    with jax.named_scope("head"):
        gap = jnp.zeros((E, 16), jnp.bfloat16)
        end = jnp.zeros((E, 80), jnp.bfloat16)
        queries, keys, values = jnp.split(project_in, 3, axis=1)
        weight = jnp.concatenate([queries, gap, values, gap, keys, end], axis=1)
        rate = head_rates[my_index]
        choice = jnp.stack([rate, my_index % rate]).astype(jnp.int32)
        head_out = head_attention(positions[0], choice, rows, fresh, weight, seq_count)

    with jax.named_scope("out"):
        gathered = lax.all_to_all(head_out, "seq", split_axis=0, concat_axis=0, tiled=True)
        gathered = gathered.reshape(E, -1)
        output = lax.dot_general(
            gathered, project_out, (((0,), (0,)), ((), ())), preferred_element_type=jnp.float32
        ).astype(jnp.bfloat16)
    return output[None]


def solution(mesh):
    in_specs = (
        P("enc", "seq", None, None, None),
        P("enc", None),
        P(),
        P(),
        P(),
        P("enc", None),
        P("enc", "seq", None),
        P(None, "seq"),
        P(),
        P(),
    )
    out_specs = P("enc", "seq", None)
    return jax.shard_map(shards, mesh=mesh, in_specs=in_specs, out_specs=out_specs, check_vma=False)
```

```python
from functools import partial

import jax
import jax.numpy as jnp
from jax import lax
from jax.experimental import pallas as pl
from jax.experimental.pallas import tpu as pltpu
from jax.sharding import PartitionSpec as P

E = 768
HEADS = 16
WIDTH = E // HEADS
SEGMENT = 512
STEP_ROWS = 512


def attend(rate, offset, table, out_ref):
    length = table.shape[1]
    loc = out_ref.shape[2]
    spread = None
    if rate > 1:
        source = lax.broadcasted_iota(jnp.int32, (128, 128 * rate), 0)
        target = lax.broadcasted_iota(jnp.int32, (128, 128 * rate), 1)
        spread = (target == offset + rate * source).astype(jnp.float32).astype(jnp.bfloat16)
    lane = lax.broadcasted_iota(jnp.int32, (SEGMENT, 128), 1)

    def segment(index, carry):
        start = index * (SEGMENT * rate) + offset
        if rate == 1:
            start = pl.multiple_of(index * SEGMENT, SEGMENT)
            rows = pl.ds(start, SEGMENT)
        else:
            rows = pl.ds(start, SEGMENT, stride=rate)
        query_value = table[0, rows, :]
        keys = table[1, rows, :].astype(jnp.bfloat16)
        with_ones = jnp.where(lane == 112, 1.0, query_value).astype(jnp.bfloat16)
        query_value = query_value.astype(jnp.bfloat16)
        for part in range(SEGMENT // 256):
            queries = query_value[part * 256 : (part + 1) * 256]
            scores = lax.dot_general(
                keys, queries, (((1,), (1,)), ((), ())), preferred_element_type=jnp.float32
            )
            top = jnp.max(scores, axis=0, keepdims=True)
            raised = jnp.exp((scores - top) * WIDTH**-0.5).astype(jnp.bfloat16)
            mixed = lax.dot_general(
                with_ones, raised, (((0,), (0,)), ((), ())), preferred_element_type=jnp.float32
            )
            result = (mixed[64:112] / mixed[112:113]).astype(jnp.bfloat16)
            if rate == 1:
                out_ref[index * (SEGMENT // loc) + part] = result
            else:
                for half in range(2):
                    wide = jnp.dot(
                        result[:, half * 128 : (half + 1) * 128],
                        spread,
                        preferred_element_type=jnp.float32,
                    ).astype(jnp.bfloat16)
                    blocks = 128 * rate // loc
                    first = (index * 4 + part * 2 + half) * blocks
                    for block in range(blocks):
                        out_ref[first + block] = wide[:, block * loc : (block + 1) * loc]
        return carry

    lax.fori_loop(0, length // (SEGMENT * rate), segment, 0)


def head_kernel(places, choice, rows_ref, fresh_ref, weight_ref, out_ref, table, fresh):
    step = pl.program_id(0)
    made = jnp.dot(rows_ref[...], weight_ref[...], preferred_element_type=jnp.float32)
    made = made.astype(jnp.bfloat16).astype(jnp.float32)
    block = pl.ds(pl.multiple_of(step * STEP_ROWS, STEP_ROWS), STEP_ROWS)
    table[0, block, :] = made[:, :128]
    table[1, block, :] = made[:, 128:]

    @pl.when(step == pl.num_programs(0) - 1)
    def _():
        made_fresh = jnp.dot(fresh_ref[...], weight_ref[...], preferred_element_type=jnp.float32)
        made_fresh = made_fresh.astype(jnp.bfloat16).astype(jnp.float32)
        fresh[0] = made_fresh[:, :128]
        fresh[1] = made_fresh[:, 128:]

        def place(group, carry):
            for inner in range(8):
                tile = group * 8 + inner
                where = places[tile]
                for side in range(2):
                    table[side, pl.ds(where, 1), :] = fresh[side, pl.ds(tile, 1), :]
            return carry

        lax.fori_loop(0, fresh.shape[1] // 8, place, 0)
        for rate in (1, 2, 4, 8):
            pl.when(choice[0] == rate)(partial(attend, rate, choice[1], table, out_ref))


def head_attention(places, choice, rows, fresh, weight, seq_count):
    length = rows.shape[0]
    loc = length // seq_count
    return pl.pallas_call(
        head_kernel,
        out_shape=jax.ShapeDtypeStruct((seq_count, WIDTH, loc), jnp.bfloat16),
        grid_spec=pltpu.PrefetchScalarGridSpec(
            num_scalar_prefetch=2,
            grid=(length // STEP_ROWS,),
            in_specs=[
                pl.BlockSpec((STEP_ROWS, E), lambda i, *_: (i, 0)),
                pl.BlockSpec(fresh.shape, lambda i, *_: (0, 0)),
                pl.BlockSpec(weight.shape, lambda i, *_: (0, 0)),
            ],
            out_specs=pl.BlockSpec((seq_count, WIDTH, loc), lambda i, *_: (0, 0, 0)),
            scratch_shapes=[
                pltpu.VMEM((2, length, 128), jnp.float32),
                pltpu.VMEM((2, fresh.shape[0], 128), jnp.float32),
            ],
        ),
        compiler_params=pltpu.CompilerParams(
            dimension_semantics=("arbitrary",), vmem_limit_bytes=58 * 1024 * 1024
        ),
        cost_estimate=pl.CostEstimate(
            flops=2 * length * E * 256, bytes_accessed=rows.size * 2, transcendentals=length * SEGMENT
        ),
    )(places, choice, rows, fresh, weight)


def spread_to(shard, axis, count, groups=None):
    copies = jnp.broadcast_to(shard[None], (count,) + shard.shape)
    return lax.all_to_all(
        copies, axis, split_axis=0, concat_axis=0, tiled=True, axis_index_groups=groups
    )


def whole_weight(conv_weight, ready):
    enc_count = lax.axis_size("enc")
    chips = enc_count // 2
    groups = [[2 * chip + core for chip in range(chips)] for core in range(2)]
    own = spread_to(conv_weight, "enc", chips, groups)
    own, ready = lax.optimization_barrier((own, ready))
    other = lax.ppermute(own, "enc", [(e, e ^ 1) for e in range(enc_count)])
    first_core = lax.axis_index("enc") % 2 == 0
    even = jnp.where(first_core, own, other)
    odd = jnp.where(first_core, other, own)
    return jnp.stack([even, odd], axis=1).reshape(-1, conv_weight.shape[1]), ready


def shards(
    tile_maps,
    conv_weight,
    norm_gain,
    norm_bias,
    tile_proj,
    positions,
    slide_cache,
    project_in,
    project_out,
    head_rates,
):
    tile_count = tile_maps.shape[1]
    side_len = tile_maps.shape[2]
    channels = tile_maps.shape[4]
    seq_count = lax.axis_size("seq")
    my_index = lax.axis_index("seq")

    with jax.named_scope("rows"):
        rows = lax.all_gather(slide_cache[0], "seq", axis=0, tiled=True)

    with jax.named_scope("encode"):
        images = tile_maps[0]
        padded = jnp.pad(images, ((0, 0), (1, 1), (1, 1), (0, 0)))
        columns = jnp.concatenate(
            [
                padded[:, row_shift : row_shift + side_len, col_shift : col_shift + side_len, :]
                for row_shift in range(3)
                for col_shift in range(3)
            ],
            axis=-1,
        )
        columns = columns.reshape(tile_count * side_len * side_len, 9 * channels)
        weight, columns = whole_weight(conv_weight, columns)
        convolved = jnp.dot(columns, weight, preferred_element_type=jnp.float32)
        activated = jnp.maximum(convolved * norm_gain + norm_bias, 0.0) + images.reshape(
            -1, channels
        ).astype(jnp.float32)
        pooled = jnp.mean(
            activated.reshape(tile_count, side_len * side_len, channels), axis=1
        ).astype(jnp.bfloat16)
        embedded = jnp.dot(pooled, tile_proj, preferred_element_type=jnp.float32).astype(
            jnp.bfloat16
        )

    with jax.named_scope("fresh"):
        fresh = lax.all_gather(embedded, "seq", axis=0, tiled=True)

    with jax.named_scope("head"):
        gap = jnp.zeros((E, 16), jnp.bfloat16)
        end = jnp.zeros((E, 80), jnp.bfloat16)
        queries, keys, values = jnp.split(project_in, 3, axis=1)
        weight = jnp.concatenate([queries, gap, values, gap, keys, end], axis=1)
        rate = head_rates[my_index]
        choice = jnp.stack([rate, my_index % rate]).astype(jnp.int32)
        head_out = head_attention(positions[0], choice, rows, fresh, weight, seq_count)

    with jax.named_scope("out"):
        gathered = lax.all_to_all(head_out, "seq", split_axis=0, concat_axis=0, tiled=True)
        gathered = gathered.reshape(E, -1)
        output = lax.dot_general(
            gathered, project_out, (((0,), (0,)), ((), ())), preferred_element_type=jnp.float32
        ).astype(jnp.bfloat16)
    return output[None]


def solution(mesh):
    in_specs = (
        P("enc", "seq", None, None, None),
        P("enc", None),
        P(),
        P(),
        P(),
        P("enc", None),
        P("enc", "seq", None),
        P(None, "seq"),
        P(),
        P(),
    )
    out_specs = P("enc", "seq", None)
    return jax.shard_map(shards, mesh=mesh, in_specs=in_specs, out_specs=out_specs, check_vma=False)
```

```python
from functools import partial

import jax
import jax.numpy as jnp
from jax import lax
from jax.experimental import pallas as pl
from jax.experimental.pallas import tpu as pltpu
from jax.sharding import PartitionSpec as P

E = 768
HEADS = 16
WIDTH = E // HEADS
SEGMENT = 512
STEP_ROWS = 512


def attend(rate, offset, table, out_ref):
    length = table.shape[1]
    loc = out_ref.shape[2]
    spread = None
    if rate > 1:
        source = lax.broadcasted_iota(jnp.int32, (128, 128 * rate), 0)
        target = lax.broadcasted_iota(jnp.int32, (128, 128 * rate), 1)
        spread = (target == offset + rate * source).astype(jnp.float32).astype(jnp.bfloat16)
    lane = lax.broadcasted_iota(jnp.int32, (SEGMENT, 128), 1)

    def segment(index, carry):
        start = index * (SEGMENT * rate) + offset
        if rate == 1:
            start = pl.multiple_of(index * SEGMENT, SEGMENT)
            rows = pl.ds(start, SEGMENT)
        else:
            rows = pl.ds(start, SEGMENT, stride=rate)
        query_value = table[0, rows, :]
        keys = table[1, rows, :].astype(jnp.bfloat16)
        with_ones = jnp.where(lane == 112, 1.0, query_value).astype(jnp.bfloat16)
        query_value = query_value.astype(jnp.bfloat16)
        for part in range(SEGMENT // 256):
            queries = query_value[part * 256 : (part + 1) * 256]
            scores = lax.dot_general(
                keys, queries, (((1,), (1,)), ((), ())), preferred_element_type=jnp.float32
            )
            top = jnp.max(scores, axis=0, keepdims=True)
            raised = jnp.exp((scores - top) * WIDTH**-0.5).astype(jnp.bfloat16)
            mixed = lax.dot_general(
                with_ones, raised, (((0,), (0,)), ((), ())), preferred_element_type=jnp.float32
            )
            result = (mixed[64:112] / mixed[112:113]).astype(jnp.bfloat16)
            if rate == 1:
                out_ref[index * (SEGMENT // loc) + part] = result
            else:
                for half in range(2):
                    wide = jnp.dot(
                        result[:, half * 128 : (half + 1) * 128],
                        spread,
                        preferred_element_type=jnp.float32,
                    ).astype(jnp.bfloat16)
                    blocks = 128 * rate // loc
                    first = (index * 4 + part * 2 + half) * blocks
                    for block in range(blocks):
                        out_ref[first + block] = wide[:, block * loc : (block + 1) * loc]
        return carry

    lax.fori_loop(0, length // (SEGMENT * rate), segment, 0)


def head_kernel(places, choice, rows_ref, fresh_ref, weight_ref, out_ref, table, fresh):
    step = pl.program_id(0)
    made = jnp.dot(rows_ref[...], weight_ref[...], preferred_element_type=jnp.float32)
    made = made.astype(jnp.bfloat16).astype(jnp.float32)
    block = pl.ds(pl.multiple_of(step * STEP_ROWS, STEP_ROWS), STEP_ROWS)
    table[0, block, :] = made[:, :128]
    table[1, block, :] = made[:, 128:]

    @pl.when(step == pl.num_programs(0) - 1)
    def _():
        made_fresh = jnp.dot(fresh_ref[...], weight_ref[...], preferred_element_type=jnp.float32)
        made_fresh = made_fresh.astype(jnp.bfloat16).astype(jnp.float32)
        fresh[0] = made_fresh[:, :128]
        fresh[1] = made_fresh[:, 128:]

        def place(group, carry):
            for inner in range(8):
                tile = group * 8 + inner
                where = places[tile]
                for side in range(2):
                    table[side, pl.ds(where, 1), :] = fresh[side, pl.ds(tile, 1), :]
            return carry

        lax.fori_loop(0, fresh.shape[1] // 8, place, 0)
        for rate in (1, 2, 4, 8):
            pl.when(choice[0] == rate)(partial(attend, rate, choice[1], table, out_ref))


def head_attention(places, choice, rows, fresh, weight, seq_count):
    length = rows.shape[0]
    loc = length // seq_count
    return pl.pallas_call(
        head_kernel,
        out_shape=jax.ShapeDtypeStruct((seq_count, WIDTH, loc), jnp.bfloat16),
        grid_spec=pltpu.PrefetchScalarGridSpec(
            num_scalar_prefetch=2,
            grid=(length // STEP_ROWS,),
            in_specs=[
                pl.BlockSpec((STEP_ROWS, E), lambda i, *_: (i, 0)),
                pl.BlockSpec(fresh.shape, lambda i, *_: (0, 0)),
                pl.BlockSpec(weight.shape, lambda i, *_: (0, 0)),
            ],
            out_specs=pl.BlockSpec((seq_count, WIDTH, loc), lambda i, *_: (0, 0, 0)),
            scratch_shapes=[
                pltpu.VMEM((2, length, 128), jnp.float32),
                pltpu.VMEM((2, fresh.shape[0], 128), jnp.float32),
            ],
        ),
        compiler_params=pltpu.CompilerParams(
            dimension_semantics=("arbitrary",), vmem_limit_bytes=24 * 1024 * 1024
        ),
        cost_estimate=pl.CostEstimate(
            flops=2 * length * E * 256, bytes_accessed=rows.size * 2, transcendentals=length * SEGMENT
        ),
    )(places, choice, rows, fresh, weight)


def spread_to(shard, axis, count, groups=None):
    copies = jnp.broadcast_to(shard[None], (count,) + shard.shape)
    return lax.all_to_all(
        copies, axis, split_axis=0, concat_axis=0, tiled=True, axis_index_groups=groups
    )


def whole_weight(conv_weight, ready):
    enc_count = lax.axis_size("enc")
    chips = enc_count // 2
    groups = [[2 * chip + core for chip in range(chips)] for core in range(2)]
    own = spread_to(conv_weight, "enc", chips, groups)
    own, ready = lax.optimization_barrier((own, ready))
    other = lax.ppermute(own, "enc", [(e, e ^ 1) for e in range(enc_count)])
    first_core = lax.axis_index("enc") % 2 == 0
    even = jnp.where(first_core, own, other)
    odd = jnp.where(first_core, other, own)
    return jnp.stack([even, odd], axis=1).reshape(-1, conv_weight.shape[1]), ready


def shards(
    tile_maps,
    conv_weight,
    norm_gain,
    norm_bias,
    tile_proj,
    positions,
    slide_cache,
    project_in,
    project_out,
    head_rates,
):
    tile_count = tile_maps.shape[1]
    side_len = tile_maps.shape[2]
    channels = tile_maps.shape[4]
    seq_count = lax.axis_size("seq")
    my_index = lax.axis_index("seq")

    with jax.named_scope("rows"):
        rows = lax.all_gather(slide_cache[0], "seq", axis=0, tiled=True)

    with jax.named_scope("choice"):
        gap = jnp.zeros((E, 16), jnp.bfloat16)
        end = jnp.zeros((E, 80), jnp.bfloat16)
        queries, keys, values = jnp.split(project_in, 3, axis=1)
        head_weight = jnp.concatenate([queries, gap, values, gap, keys, end], axis=1)
        rate = head_rates[my_index]
        choice = jnp.stack([rate, my_index % rate]).astype(jnp.int32)

    with jax.named_scope("encode"):
        images = tile_maps[0]
        padded = jnp.pad(images, ((0, 0), (1, 1), (1, 1), (0, 0)))
        columns = jnp.concatenate(
            [
                padded[:, row_shift : row_shift + side_len, col_shift : col_shift + side_len, :]
                for row_shift in range(3)
                for col_shift in range(3)
            ],
            axis=-1,
        )
        columns = columns.reshape(tile_count * side_len * side_len, 9 * channels)
        weight, (columns, head_weight, choice) = whole_weight(
            conv_weight, (columns, head_weight, choice)
        )
        convolved = jnp.dot(columns, weight, preferred_element_type=jnp.float32)
        activated = jnp.maximum(convolved * norm_gain + norm_bias, 0.0) + images.reshape(
            -1, channels
        ).astype(jnp.float32)
        pooled = jnp.mean(
            activated.reshape(tile_count, side_len * side_len, channels), axis=1
        ).astype(jnp.bfloat16)
        embedded = jnp.dot(pooled, tile_proj, preferred_element_type=jnp.float32).astype(
            jnp.bfloat16
        )

    with jax.named_scope("fresh"):
        fresh = lax.all_gather(embedded, "seq", axis=0, tiled=True)

    with jax.named_scope("head"):
        head_out = head_attention(positions[0], choice, rows, fresh, head_weight, seq_count)

    with jax.named_scope("out"):
        gathered = lax.all_to_all(head_out, "seq", split_axis=0, concat_axis=0, tiled=True)
        gathered = gathered.reshape(E, -1)
        output = lax.dot_general(
            gathered, project_out, (((0,), (0,)), ((), ())), preferred_element_type=jnp.float32
        ).astype(jnp.bfloat16)
    return output[None]


def solution(mesh):
    in_specs = (
        P("enc", "seq", None, None, None),
        P("enc", None),
        P(),
        P(),
        P(),
        P("enc", None),
        P("enc", "seq", None),
        P(None, "seq"),
        P(),
        P(),
    )
    out_specs = P("enc", "seq", None)
    return jax.shard_map(shards, mesh=mesh, in_specs=in_specs, out_specs=out_specs, check_vma=False)
```

```python
import math
from functools import partial

import jax
import jax.numpy as jnp
from jax import lax
from jax.experimental import pallas as pl
from jax.experimental.pallas import tpu as pltpu
from jax.sharding import PartitionSpec as P

E = 768
HEADS = 16
WIDTH = E // HEADS
SEGMENT = 512
STEP_ROWS = 512
SCALE = WIDTH**-0.5 * math.log2(math.e)


def attend(rate, offset, table, out_ref):
    length = table.shape[1]
    loc = out_ref.shape[2]
    spread = None
    if rate > 1:
        source = lax.broadcasted_iota(jnp.int32, (128, 128 * rate), 0)
        target = lax.broadcasted_iota(jnp.int32, (128, 128 * rate), 1)
        spread = (target == offset + rate * source).astype(jnp.float32).astype(jnp.bfloat16)
    lane = lax.broadcasted_iota(jnp.int32, (SEGMENT, 128), 1)

    def segment(index, carry):
        start = index * (SEGMENT * rate) + offset
        if rate == 1:
            start = pl.multiple_of(index * SEGMENT, SEGMENT)
            rows = pl.ds(start, SEGMENT)
        else:
            rows = pl.ds(start, SEGMENT, stride=rate)
        query_value = table[0, rows, :]
        keys = table[1, rows, :].astype(jnp.bfloat16)
        with_ones = jnp.where(lane == 112, 1.0, query_value).astype(jnp.bfloat16)
        query_value = query_value.astype(jnp.bfloat16)
        for part in range(SEGMENT // 256):
            queries = query_value[part * 256 : (part + 1) * 256]
            scores = lax.dot_general(
                keys, queries, (((1,), (1,)), ((), ())), preferred_element_type=jnp.float32
            )
            top = jnp.max(scores, axis=0, keepdims=True)
            raised = jnp.exp2((scores - top) * SCALE).astype(jnp.bfloat16)
            mixed = lax.dot_general(
                with_ones, raised, (((0,), (0,)), ((), ())), preferred_element_type=jnp.float32
            )
            result = (mixed[64:112] / mixed[112:113]).astype(jnp.bfloat16)
            if rate == 1:
                out_ref[index * (SEGMENT // loc) + part] = result
            else:
                for half in range(2):
                    wide = jnp.dot(
                        result[:, half * 128 : (half + 1) * 128],
                        spread,
                        preferred_element_type=jnp.float32,
                    ).astype(jnp.bfloat16)
                    blocks = 128 * rate // loc
                    first = (index * 4 + part * 2 + half) * blocks
                    for block in range(blocks):
                        out_ref[first + block] = wide[:, block * loc : (block + 1) * loc]
        return carry

    lax.fori_loop(0, length // (SEGMENT * rate), segment, 0, unroll=2 if rate < 8 else 1)


def head_kernel(
    places, choice, rows_ref, fresh_ref, weight_ref, out_ref, table, fresh, held, arrived
):
    chunks = held.shape[0]

    def arrival(chunk):
        first = pl.multiple_of(chunk * STEP_ROWS, STEP_ROWS)
        return pltpu.make_async_copy(
            rows_ref.at[pl.ds(first, STEP_ROWS)], held.at[chunk], arrived.at[chunk]
        )

    for chunk in range(chunks):
        arrival(chunk).start()
    made_fresh = jnp.dot(fresh_ref[...], weight_ref[...], preferred_element_type=jnp.float32)
    made_fresh = made_fresh.astype(jnp.bfloat16).astype(jnp.float32)
    fresh[0] = made_fresh[:, :128]
    fresh[1] = made_fresh[:, 128:]

    def project(chunk, carry):
        arrival(chunk).wait()
        made = jnp.dot(held[chunk], weight_ref[...], preferred_element_type=jnp.float32)
        made = made.astype(jnp.bfloat16).astype(jnp.float32)
        block = pl.ds(pl.multiple_of(chunk * STEP_ROWS, STEP_ROWS), STEP_ROWS)
        table[0, block, :] = made[:, :128]
        table[1, block, :] = made[:, 128:]
        return carry

    lax.fori_loop(0, chunks, project, 0)

    def place(group, carry):
        for inner in range(8):
            tile = group * 8 + inner
            where = places[tile]
            for side in range(2):
                table[side, pl.ds(where, 1), :] = fresh[side, pl.ds(tile, 1), :]
        return carry

    lax.fori_loop(0, fresh.shape[1] // 8, place, 0)
    for rate in (1, 2, 4, 8):
        pl.when(choice[0] == rate)(partial(attend, rate, choice[1], table, out_ref))


def head_attention(places, choice, rows, fresh, weight, seq_count):
    length = rows.shape[0]
    loc = length // seq_count
    chunks = length // STEP_ROWS
    return pl.pallas_call(
        head_kernel,
        out_shape=jax.ShapeDtypeStruct((seq_count, WIDTH, loc), jnp.bfloat16),
        in_specs=[
            pl.BlockSpec(memory_space=pltpu.SMEM),
            pl.BlockSpec(memory_space=pltpu.SMEM),
            pl.BlockSpec(memory_space=pltpu.HBM),
            pl.BlockSpec(memory_space=pltpu.VMEM),
            pl.BlockSpec(memory_space=pltpu.VMEM),
        ],
        out_specs=pl.BlockSpec(memory_space=pltpu.VMEM),
        scratch_shapes=[
            pltpu.VMEM((2, length, 128), jnp.float32),
            pltpu.VMEM((2, fresh.shape[0], 128), jnp.float32),
            pltpu.VMEM((chunks, STEP_ROWS, E), jnp.bfloat16),
            pltpu.SemaphoreType.DMA((chunks,)),
        ],
        compiler_params=pltpu.CompilerParams(vmem_limit_bytes=24 * 1024 * 1024),
        cost_estimate=pl.CostEstimate(
            flops=2 * length * E * 256, bytes_accessed=rows.size * 2, transcendentals=length * SEGMENT
        ),
    )(places, choice, rows, fresh, weight)


def regroup_kernel(shard, core, columns_ref, own_ref, other_ref):
    columns = columns_ref[...]
    count = columns.shape[1] // shard
    even, odd = (
        jnp.concatenate(
            [columns[:, j * shard : (j + 1) * shard] for j in range(first, count, 2)], axis=1
        )
        for first in range(2)
    )

    @pl.when(core[0] == 0)
    def _():
        own_ref[...] = even
        other_ref[...] = odd

    @pl.when(core[0] == 1)
    def _():
        own_ref[...] = odd
        other_ref[...] = even


def regroup(core, columns, shard):
    rows, depth = columns.shape
    half = jax.ShapeDtypeStruct((rows, depth // 2), columns.dtype)
    block = 128
    return pl.pallas_call(
        partial(regroup_kernel, shard),
        out_shape=(half, half),
        grid_spec=pltpu.PrefetchScalarGridSpec(
            num_scalar_prefetch=1,
            grid=(rows // block,),
            in_specs=[pl.BlockSpec((block, depth), lambda i, *_: (i, 0))],
            out_specs=[pl.BlockSpec((block, depth // 2), lambda i, *_: (i, 0))] * 2,
        ),
        compiler_params=pltpu.CompilerParams(vmem_limit_bytes=24 * 1024 * 1024),
        cost_estimate=pl.CostEstimate(
            flops=0, bytes_accessed=columns.size * 4, transcendentals=0
        ),
    )(core, columns)


def spread_to(shard, axis, count, groups=None):
    copies = jnp.broadcast_to(shard[None], (count,) + shard.shape)
    return lax.all_to_all(
        copies, axis, split_axis=0, concat_axis=0, tiled=True, axis_index_groups=groups
    )


def convolve(conv_weight, columns, ready):
    enc_count = lax.axis_size("enc")
    chips = enc_count // 2
    shard, channels = conv_weight.shape
    groups = [[2 * chip + core for chip in range(chips)] for core in range(2)]
    own = spread_to(conv_weight, "enc", chips, groups)
    core = (lax.axis_index("enc") % 2).astype(jnp.int32).reshape(1)
    own_columns, other_columns = regroup(core, columns, shard)
    own, own_columns, other_columns, ready = lax.optimization_barrier(
        (own, own_columns, other_columns, ready)
    )
    other = lax.ppermute(own, "enc", [(e, e ^ 1) for e in range(enc_count)])
    first = jnp.dot(
        own_columns, own.reshape(-1, channels), preferred_element_type=jnp.float32
    )
    second = jnp.dot(
        other_columns, other.reshape(-1, channels), preferred_element_type=jnp.float32
    )
    return first + second, ready


def shards(
    tile_maps,
    conv_weight,
    norm_gain,
    norm_bias,
    tile_proj,
    positions,
    slide_cache,
    project_in,
    project_out,
    head_rates,
):
    tile_count = tile_maps.shape[1]
    side_len = tile_maps.shape[2]
    channels = tile_maps.shape[4]
    seq_count = lax.axis_size("seq")
    my_index = lax.axis_index("seq")

    with jax.named_scope("rows"):
        rows = lax.all_gather(slide_cache[0], "seq", axis=0, tiled=True)

    with jax.named_scope("choice"):
        gap = jnp.zeros((E, 16), jnp.bfloat16)
        end = jnp.zeros((E, 80), jnp.bfloat16)
        queries, keys, values = jnp.split(project_in, 3, axis=1)
        head_weight = jnp.concatenate([queries, gap, values, gap, keys, end], axis=1)
        rate = head_rates[my_index]
        choice = jnp.stack([rate, my_index % rate]).astype(jnp.int32)

    with jax.named_scope("encode"):
        images = tile_maps[0]
        padded = jnp.pad(images, ((0, 0), (1, 1), (1, 1), (0, 0)))
        columns = jnp.concatenate(
            [
                padded[:, row_shift : row_shift + side_len, col_shift : col_shift + side_len, :]
                for row_shift in range(3)
                for col_shift in range(3)
            ],
            axis=-1,
        )
        columns = columns.reshape(tile_count * side_len * side_len, 9 * channels)
        convolved, (head_weight, choice) = convolve(conv_weight, columns, (head_weight, choice))
        activated = jnp.maximum(convolved * norm_gain + norm_bias, 0.0) + images.reshape(
            -1, channels
        ).astype(jnp.float32)
        pooled = jnp.mean(
            activated.reshape(tile_count, side_len * side_len, channels), axis=1
        ).astype(jnp.bfloat16)
        embedded = jnp.dot(pooled, tile_proj, preferred_element_type=jnp.float32).astype(
            jnp.bfloat16
        )

    with jax.named_scope("fresh"):
        fresh = lax.all_gather(embedded, "seq", axis=0, tiled=True)

    with jax.named_scope("head"):
        head_out = head_attention(positions[0], choice, rows, fresh, head_weight, seq_count)

    with jax.named_scope("out"):
        gathered = lax.all_to_all(head_out, "seq", split_axis=0, concat_axis=0, tiled=True)
        gathered = gathered.reshape(E, -1)
        output = lax.dot_general(
            gathered, project_out, (((0,), (0,)), ((), ())), preferred_element_type=jnp.float32
        ).astype(jnp.bfloat16)
    return output[None]


def solution(mesh):
    in_specs = (
        P("enc", "seq", None, None, None),
        P("enc", None),
        P(),
        P(),
        P(),
        P("enc", None),
        P("enc", "seq", None),
        P(None, "seq"),
        P(),
        P(),
    )
    out_specs = P("enc", "seq", None)
    return jax.shard_map(shards, mesh=mesh, in_specs=in_specs, out_specs=out_specs, check_vma=False)
```

```python
import math
from functools import partial

import jax
import jax.numpy as jnp
from jax import lax
from jax.experimental import pallas as pl
from jax.experimental.pallas import tpu as pltpu
from jax.sharding import PartitionSpec as P

E = 768
HEADS = 16
WIDTH = E // HEADS
SEGMENT = 512
STEP_ROWS = 1024
SCALE = WIDTH**-0.5 * math.log2(math.e)


def attend(rate, offset, table, out_ref):
    length = table.shape[1]
    loc = out_ref.shape[2]
    spread = None
    if rate > 1:
        source = lax.broadcasted_iota(jnp.int32, (128, 128 * rate), 0)
        target = lax.broadcasted_iota(jnp.int32, (128, 128 * rate), 1)
        spread = (target == offset + rate * source).astype(jnp.float32).astype(jnp.bfloat16)
    lane = lax.broadcasted_iota(jnp.int32, (SEGMENT, 128), 1)
    def load(index):
        start = index * (SEGMENT * rate) + offset
        if rate == 1:
            rows = pl.ds(pl.multiple_of(index * SEGMENT, SEGMENT), SEGMENT)
        else:
            rows = pl.ds(start, SEGMENT, stride=rate)
        query_value = table[0, rows, :]
        keys = table[1, rows, :].astype(jnp.bfloat16)
        with_ones = jnp.where(lane == 112, 1.0, query_value).astype(jnp.bfloat16)
        return query_value.astype(jnp.bfloat16), keys, with_ones

    def score(loaded, part):
        queries, keys, _ = loaded
        return lax.dot_general(
            keys,
            queries[part * 512 : (part + 1) * 512],
            (((1,), (1,)), ((), ())),
            preferred_element_type=jnp.float32,
        )

    def finish(index, part, loaded, scores):
        top = jnp.max(scores, axis=0, keepdims=True)
        raised = jnp.exp2((scores - top) * SCALE).astype(jnp.bfloat16)
        mixed = lax.dot_general(
            loaded[2], raised, (((0,), (0,)), ((), ())), preferred_element_type=jnp.float32
        )
        result = (mixed[64:112] / mixed[112:113]).astype(jnp.bfloat16)
        if rate == 1:
            for block in range(512 // loc):
                out_ref[index * (SEGMENT // loc) + part * (512 // loc) + block] = result[
                    :, block * loc : (block + 1) * loc
                ]
            return
        blocks = 128 * rate // loc
        for piece in range(512 // 128):
            wide = jnp.dot(
                result[:, piece * 128 : (piece + 1) * 128],
                spread,
                preferred_element_type=jnp.float32,
            ).astype(jnp.bfloat16)
            first = (index * 4 + part * (512 // 128) + piece) * blocks
            for block in range(blocks):
                out_ref[first + block] = wide[:, block * loc : (block + 1) * loc]

    segments = length // (SEGMENT * rate)
    together = min(segments, 4)

    def group(step, carry):
        work = []
        for inner in range(together):
            index = step * together + inner
            loaded = load(index)
            work += [(index, part, loaded) for part in range(SEGMENT // 512)]
        ahead = [score(loaded, part) for _, part, loaded in work[:1]]
        for number, (index, part, loaded) in enumerate(work):
            if number + 1 < len(work):
                _, next_part, next_loaded = work[number + 1]
                ahead.append(score(next_loaded, next_part))
            finish(index, part, loaded, ahead[number])
        return carry

    lax.fori_loop(0, segments // together, group, 0)


def head_kernel(
    places, choice, rows_ref, fresh_ref, weight_ref, out_ref, table, fresh, held, arrived
):
    chunks = held.shape[0]

    def arrival(chunk):
        first = pl.multiple_of(chunk * STEP_ROWS, STEP_ROWS)
        return pltpu.make_async_copy(
            rows_ref.at[pl.ds(first, STEP_ROWS)], held.at[chunk], arrived.at[chunk]
        )

    for chunk in range(chunks):
        arrival(chunk).start()
    made_fresh = jnp.dot(fresh_ref[...], weight_ref[...], preferred_element_type=jnp.float32)
    made_fresh = made_fresh.astype(jnp.bfloat16).astype(jnp.float32)
    fresh[0] = made_fresh[:, :128]
    fresh[1] = made_fresh[:, 128:]

    def project(chunk, carry):
        arrival(chunk).wait()
        made = jnp.dot(held[chunk], weight_ref[...], preferred_element_type=jnp.float32)
        made = made.astype(jnp.bfloat16).astype(jnp.float32)
        block = pl.ds(pl.multiple_of(chunk * STEP_ROWS, STEP_ROWS), STEP_ROWS)
        table[0, block, :] = made[:, :128]
        table[1, block, :] = made[:, 128:]
        return carry

    lax.fori_loop(0, chunks, project, 0)

    def place(group, carry):
        for inner in range(8):
            tile = group * 8 + inner
            where = places[tile]
            for side in range(2):
                table[side, pl.ds(where, 1), :] = fresh[side, pl.ds(tile, 1), :]
        return carry

    lax.fori_loop(0, fresh.shape[1] // 8, place, 0)
    for rate in (1, 2, 4, 8):
        pl.when(choice[0] == rate)(partial(attend, rate, choice[1], table, out_ref))


def head_attention(places, choice, rows, fresh, weight, seq_count):
    length = rows.shape[0]
    loc = length // seq_count
    chunks = length // STEP_ROWS
    return pl.pallas_call(
        head_kernel,
        out_shape=jax.ShapeDtypeStruct((seq_count, WIDTH, loc), jnp.bfloat16),
        in_specs=[
            pl.BlockSpec(memory_space=pltpu.SMEM),
            pl.BlockSpec(memory_space=pltpu.SMEM),
            pl.BlockSpec(memory_space=pltpu.HBM),
            pl.BlockSpec(memory_space=pltpu.VMEM),
            pl.BlockSpec(memory_space=pltpu.VMEM),
        ],
        out_specs=pl.BlockSpec(memory_space=pltpu.VMEM),
        scratch_shapes=[
            pltpu.VMEM((2, length, 128), jnp.float32),
            pltpu.VMEM((2, fresh.shape[0], 128), jnp.float32),
            pltpu.VMEM((chunks, STEP_ROWS, E), jnp.bfloat16),
            pltpu.SemaphoreType.DMA((chunks,)),
        ],
        compiler_params=pltpu.CompilerParams(vmem_limit_bytes=48 * 1024 * 1024),
        cost_estimate=pl.CostEstimate(
            flops=2 * length * E * 256, bytes_accessed=0, transcendentals=0
        ),
    )(places, choice, rows, fresh, weight)


def regroup_kernel(shard, core, columns_ref, own_ref, other_ref):
    columns = columns_ref[...]
    count = columns.shape[1] // shard
    even, odd = (
        jnp.concatenate(
            [columns[:, j * shard : (j + 1) * shard] for j in range(first, count, 2)], axis=1
        )
        for first in range(2)
    )

    @pl.when(core[0] == 0)
    def _():
        own_ref[...] = even
        other_ref[...] = odd

    @pl.when(core[0] == 1)
    def _():
        own_ref[...] = odd
        other_ref[...] = even


def regroup(core, columns, shard):
    rows, depth = columns.shape
    half = jax.ShapeDtypeStruct((rows, depth // 2), columns.dtype)
    block = 128
    return pl.pallas_call(
        partial(regroup_kernel, shard),
        out_shape=(half, half),
        grid_spec=pltpu.PrefetchScalarGridSpec(
            num_scalar_prefetch=1,
            grid=(rows // block,),
            in_specs=[pl.BlockSpec((block, depth), lambda i, *_: (i, 0))],
            out_specs=[pl.BlockSpec((block, depth // 2), lambda i, *_: (i, 0))] * 2,
        ),
        compiler_params=pltpu.CompilerParams(vmem_limit_bytes=24 * 1024 * 1024),
        cost_estimate=pl.CostEstimate(
            flops=0, bytes_accessed=columns.size * 4, transcendentals=0
        ),
    )(core, columns)


def spread_to(shard, axis, count, groups=None):
    copies = jnp.broadcast_to(shard[None], (count,) + shard.shape)
    return lax.all_to_all(
        copies, axis, split_axis=0, concat_axis=0, tiled=True, axis_index_groups=groups
    )


def convolve(conv_weight, columns, ready):
    enc_count = lax.axis_size("enc")
    chips = enc_count // 2
    shard, channels = conv_weight.shape
    groups = [[2 * chip + core for chip in range(chips)] for core in range(2)]
    own = spread_to(conv_weight, "enc", chips, groups)
    core = (lax.axis_index("enc") % 2).astype(jnp.int32).reshape(1)
    own_columns, other_columns = regroup(core, columns, shard)
    own, own_columns, other_columns, ready = lax.optimization_barrier(
        (own, own_columns, other_columns, ready)
    )
    other = lax.ppermute(own, "enc", [(e, e ^ 1) for e in range(enc_count)])
    first = jnp.dot(
        own_columns, own.reshape(-1, channels), preferred_element_type=jnp.float32
    )
    second = jnp.dot(
        other_columns, other.reshape(-1, channels), preferred_element_type=jnp.float32
    )
    return first + second, ready


def shards(
    tile_maps,
    conv_weight,
    norm_gain,
    norm_bias,
    tile_proj,
    positions,
    slide_cache,
    project_in,
    project_out,
    head_rates,
):
    tile_count = tile_maps.shape[1]
    side_len = tile_maps.shape[2]
    channels = tile_maps.shape[4]
    seq_count = lax.axis_size("seq")
    my_index = lax.axis_index("seq")

    with jax.named_scope("rows"):
        rows = lax.all_gather(slide_cache[0], "seq", axis=0, tiled=True)

    with jax.named_scope("choice"):
        gap = jnp.zeros((E, 16), jnp.bfloat16)
        end = jnp.zeros((E, 80), jnp.bfloat16)
        queries, keys, values = jnp.split(project_in, 3, axis=1)
        head_weight = jnp.concatenate([queries, gap, values, gap, keys, end], axis=1)
        rate = head_rates[my_index]
        choice = jnp.stack([rate, my_index % rate]).astype(jnp.int32)

    with jax.named_scope("encode"):
        images = tile_maps[0]
        padded = jnp.pad(images, ((0, 0), (1, 1), (1, 1), (0, 0)))
        columns = jnp.concatenate(
            [
                padded[:, row_shift : row_shift + side_len, col_shift : col_shift + side_len, :]
                for row_shift in range(3)
                for col_shift in range(3)
            ],
            axis=-1,
        )
        columns = columns.reshape(tile_count * side_len * side_len, 9 * channels)
        convolved, (head_weight, choice) = convolve(conv_weight, columns, (head_weight, choice))
        activated = jnp.maximum(convolved * norm_gain + norm_bias, 0.0) + images.reshape(
            -1, channels
        ).astype(jnp.float32)
        pooled = jnp.mean(
            activated.reshape(tile_count, side_len * side_len, channels), axis=1
        ).astype(jnp.bfloat16)
        embedded = jnp.dot(pooled, tile_proj, preferred_element_type=jnp.float32).astype(
            jnp.bfloat16
        )

    with jax.named_scope("fresh"):
        fresh = lax.all_gather(embedded, "seq", axis=0, tiled=True)

    with jax.named_scope("head"):
        head_out = head_attention(positions[0], choice, rows, fresh, head_weight, seq_count)

    with jax.named_scope("out"):
        gathered = lax.all_to_all(head_out, "seq", split_axis=0, concat_axis=0, tiled=True)
        gathered = gathered.reshape(E, -1)
        output = lax.dot_general(
            gathered, project_out, (((0,), (0,)), ((), ())), preferred_element_type=jnp.float32
        ).astype(jnp.bfloat16)
    return output[None]


def solution(mesh):
    in_specs = (
        P("enc", "seq", None, None, None),
        P("enc", None),
        P(),
        P(),
        P(),
        P("enc", None),
        P("enc", "seq", None),
        P(None, "seq"),
        P(),
        P(),
    )
    out_specs = P("enc", "seq", None)
    return jax.shard_map(shards, mesh=mesh, in_specs=in_specs, out_specs=out_specs, check_vma=False)
```

```python
import math
from functools import partial

import jax
import jax.numpy as jnp
from jax import lax
from jax.experimental import pallas as pl
from jax.experimental.pallas import tpu as pltpu
from jax.sharding import PartitionSpec as P

E = 768
HEADS = 16
WIDTH = E // HEADS
SEGMENT = 512
STEP_BLOCKS = 4
TAIL = 16
SCALE = WIDTH**-0.5 * math.log2(math.e)


def attend(rate, offset, table, out_ref):
    length = table.shape[1]
    loc = out_ref.shape[2]
    spread = None
    if rate > 1:
        source = lax.broadcasted_iota(jnp.int32, (128, 128 * rate), 0)
        target = lax.broadcasted_iota(jnp.int32, (128, 128 * rate), 1)
        spread = (target == offset + rate * source).astype(jnp.float32).astype(jnp.bfloat16)
    lane = lax.broadcasted_iota(jnp.int32, (SEGMENT, 128), 1)
    def load(index):
        start = index * (SEGMENT * rate) + offset
        if rate == 1:
            rows = pl.ds(pl.multiple_of(index * SEGMENT, SEGMENT), SEGMENT)
        else:
            rows = pl.ds(start, SEGMENT, stride=rate)
        query_value = table[0, rows, :]
        keys = table[1, rows, :].astype(jnp.bfloat16)
        with_ones = jnp.where(lane == 112, 1.0, query_value).astype(jnp.bfloat16)
        return query_value.astype(jnp.bfloat16), keys, with_ones

    def score(loaded, part):
        queries, keys, _ = loaded
        return lax.dot_general(
            keys,
            queries[part * 512 : (part + 1) * 512],
            (((1,), (1,)), ((), ())),
            preferred_element_type=jnp.float32,
        )

    def finish(index, part, loaded, scores):
        top = jnp.max(scores, axis=0, keepdims=True)
        raised = jnp.exp2((scores - top) * SCALE).astype(jnp.bfloat16)
        mixed = lax.dot_general(
            loaded[2], raised, (((0,), (0,)), ((), ())), preferred_element_type=jnp.float32
        )
        result = (mixed[64:112] / mixed[112:113]).astype(jnp.bfloat16)
        if rate == 1:
            for block in range(512 // loc):
                out_ref[index * (SEGMENT // loc) + part * (512 // loc) + block] = result[
                    :, block * loc : (block + 1) * loc
                ]
            return
        blocks = 128 * rate // loc
        for piece in range(512 // 128):
            wide = jnp.dot(
                result[:, piece * 128 : (piece + 1) * 128],
                spread,
                preferred_element_type=jnp.float32,
            ).astype(jnp.bfloat16)
            first = (index * 4 + part * (512 // 128) + piece) * blocks
            for block in range(blocks):
                out_ref[first + block] = wide[:, block * loc : (block + 1) * loc]

    segments = length // (SEGMENT * rate)
    together = min(segments, 4)

    def group(step, carry):
        work = []
        for inner in range(together):
            index = step * together + inner
            loaded = load(index)
            work += [(index, part, loaded) for part in range(SEGMENT // 512)]
        ahead = [score(loaded, part) for _, part, loaded in work[:1]]
        for number, (index, part, loaded) in enumerate(work):
            if number + 1 < len(work):
                _, next_part, next_loaded = work[number + 1]
                ahead.append(score(next_loaded, next_part))
            finish(index, part, loaded, ahead[number])
        return carry

    lax.fori_loop(0, segments // together, group, 0)


def head_kernel(
    places, choice, rows_ref, tail_ref, weight_ref, out_ref, table, fresh, held, arrived
):
    kept = rows_ref.shape[1]
    tiles = fresh.shape[1] // held.shape[0]
    loc = held.shape[1]
    step_rows = STEP_BLOCKS * loc
    chunks = held.shape[0] // STEP_BLOCKS

    def arrivals(chunk):
        blocks = pl.ds(chunk * STEP_BLOCKS, STEP_BLOCKS)
        return (
            pltpu.make_async_copy(
                rows_ref.at[blocks], held.at[blocks, pl.ds(0, kept)], arrived.at[chunk, 0]
            ),
            pltpu.make_async_copy(
                tail_ref.at[blocks, pl.ds(tiles, loc - kept)],
                held.at[blocks, pl.ds(kept, loc - kept)],
                arrived.at[chunk, 1],
            ),
        )

    for chunk in range(chunks):
        for copy in arrivals(chunk):
            copy.start()
    made_fresh = jnp.dot(
        tail_ref[:, :tiles, :].reshape(-1, E), weight_ref[...], preferred_element_type=jnp.float32
    )
    made_fresh = made_fresh.astype(jnp.bfloat16).astype(jnp.float32)
    fresh[0] = made_fresh[:, :128]
    fresh[1] = made_fresh[:, 128:]

    def project(chunk, carry):
        for copy in arrivals(chunk):
            copy.wait()
        rows = held[pl.ds(chunk * STEP_BLOCKS, STEP_BLOCKS)].reshape(step_rows, E)
        made = jnp.dot(rows, weight_ref[...], preferred_element_type=jnp.float32)
        made = made.astype(jnp.bfloat16).astype(jnp.float32)
        block = pl.ds(pl.multiple_of(chunk * step_rows, step_rows), step_rows)
        table[0, block, :] = made[:, :128]
        table[1, block, :] = made[:, 128:]
        return carry

    lax.fori_loop(0, chunks, project, 0)

    def place(group, carry):
        for inner in range(8):
            tile = group * 8 + inner
            where = places[tile]
            for side in range(2):
                table[side, pl.ds(where, 1), :] = fresh[side, pl.ds(tile, 1), :]
        return carry

    lax.fori_loop(0, fresh.shape[1] // 8, place, 0)
    for rate in (1, 2, 4, 8):
        pl.when(choice[0] == rate)(partial(attend, rate, choice[1], table, out_ref))


def head_attention(places, choice, rows, tail, weight, loc):
    blocks = rows.shape[0]
    length = blocks * loc
    new_rows = blocks * (tail.shape[1] - (loc - rows.shape[1]))
    return pl.pallas_call(
        head_kernel,
        out_shape=jax.ShapeDtypeStruct((blocks, WIDTH, loc), jnp.bfloat16),
        in_specs=[
            pl.BlockSpec(memory_space=pltpu.SMEM),
            pl.BlockSpec(memory_space=pltpu.SMEM),
            pl.BlockSpec(memory_space=pltpu.HBM),
            pl.BlockSpec(memory_space=pltpu.VMEM),
            pl.BlockSpec(memory_space=pltpu.VMEM),
        ],
        out_specs=pl.BlockSpec(memory_space=pltpu.VMEM),
        scratch_shapes=[
            pltpu.VMEM((2, length, 128), jnp.float32),
            pltpu.VMEM((2, new_rows, 128), jnp.float32),
            pltpu.VMEM((blocks, loc, E), jnp.bfloat16),
            pltpu.SemaphoreType.DMA((blocks // STEP_BLOCKS, 2)),
        ],
        compiler_params=pltpu.CompilerParams(vmem_limit_bytes=48 * 1024 * 1024),
        cost_estimate=pl.CostEstimate(
            flops=2 * length * E * 256, bytes_accessed=0, transcendentals=0
        ),
    )(places, choice, rows, tail, weight)


def regroup_kernel(shard, core, columns_ref, own_ref, other_ref):
    columns = columns_ref[...]
    count = columns.shape[1] // shard
    even, odd = (
        jnp.concatenate(
            [columns[:, j * shard : (j + 1) * shard] for j in range(first, count, 2)], axis=1
        )
        for first in range(2)
    )

    @pl.when(core[0] == 0)
    def _():
        own_ref[...] = even
        other_ref[...] = odd

    @pl.when(core[0] == 1)
    def _():
        own_ref[...] = odd
        other_ref[...] = even


def regroup(core, columns, shard):
    rows, depth = columns.shape
    half = jax.ShapeDtypeStruct((rows, depth // 2), columns.dtype)
    block = 128
    return pl.pallas_call(
        partial(regroup_kernel, shard),
        out_shape=(half, half),
        grid_spec=pltpu.PrefetchScalarGridSpec(
            num_scalar_prefetch=1,
            grid=(rows // block,),
            in_specs=[pl.BlockSpec((block, depth), lambda i, *_: (i, 0))],
            out_specs=[pl.BlockSpec((block, depth // 2), lambda i, *_: (i, 0))] * 2,
        ),
        compiler_params=pltpu.CompilerParams(vmem_limit_bytes=24 * 1024 * 1024),
        cost_estimate=pl.CostEstimate(
            flops=0, bytes_accessed=columns.size * 4, transcendentals=0
        ),
    )(core, columns)


def spread_to(shard, axis, count, groups=None):
    copies = jnp.broadcast_to(shard[None], (count,) + shard.shape)
    return lax.all_to_all(
        copies, axis, split_axis=0, concat_axis=0, tiled=True, axis_index_groups=groups
    )


def convolve(conv_weight, columns, ready):
    enc_count = lax.axis_size("enc")
    chips = enc_count // 2
    shard, channels = conv_weight.shape
    groups = [[2 * chip + core for chip in range(chips)] for core in range(2)]
    own = spread_to(conv_weight, "enc", chips, groups)
    core = (lax.axis_index("enc") % 2).astype(jnp.int32).reshape(1)
    own_columns, other_columns = regroup(core, columns, shard)
    own, own_columns, other_columns, ready = lax.optimization_barrier(
        (own, own_columns, other_columns, ready)
    )
    other = lax.ppermute(own, "enc", [(e, e ^ 1) for e in range(enc_count)])
    first = jnp.dot(
        own_columns, own.reshape(-1, channels), preferred_element_type=jnp.float32
    )
    second = jnp.dot(
        other_columns, other.reshape(-1, channels), preferred_element_type=jnp.float32
    )
    return first + second, ready


def shards(
    tile_maps,
    conv_weight,
    norm_gain,
    norm_bias,
    tile_proj,
    positions,
    slide_cache,
    project_in,
    project_out,
    head_rates,
):
    tile_count = tile_maps.shape[1]
    side_len = tile_maps.shape[2]
    channels = tile_maps.shape[4]
    my_index = lax.axis_index("seq")

    with jax.named_scope("rows"):
        loc = slide_cache.shape[1]
        rows = lax.all_gather(slide_cache[0, : loc - TAIL], "seq", axis=0, tiled=False)

    with jax.named_scope("choice"):
        gap = jnp.zeros((E, 16), jnp.bfloat16)
        end = jnp.zeros((E, 80), jnp.bfloat16)
        queries, keys, values = jnp.split(project_in, 3, axis=1)
        head_weight = jnp.concatenate([queries, gap, values, gap, keys, end], axis=1)
        rate = head_rates[my_index]
        choice = jnp.stack([rate, my_index % rate]).astype(jnp.int32)

    with jax.named_scope("encode"):
        images = tile_maps[0]
        padded = jnp.pad(images, ((0, 0), (1, 1), (1, 1), (0, 0)))
        columns = jnp.concatenate(
            [
                padded[:, row_shift : row_shift + side_len, col_shift : col_shift + side_len, :]
                for row_shift in range(3)
                for col_shift in range(3)
            ],
            axis=-1,
        )
        columns = columns.reshape(tile_count * side_len * side_len, 9 * channels)
        convolved, (head_weight, choice) = convolve(conv_weight, columns, (head_weight, choice))
        activated = jnp.maximum(convolved * norm_gain + norm_bias, 0.0) + images.reshape(
            -1, channels
        ).astype(jnp.float32)
        pooled = jnp.mean(
            activated.reshape(tile_count, side_len * side_len, channels), axis=1
        ).astype(jnp.bfloat16)
        embedded = jnp.dot(pooled, tile_proj, preferred_element_type=jnp.float32).astype(
            jnp.bfloat16
        )

    with jax.named_scope("fresh"):
        tail = jnp.concatenate([embedded, slide_cache[0, loc - TAIL :]], axis=0)
        tail = lax.all_gather(tail, "seq", axis=0, tiled=False)

    with jax.named_scope("head"):
        head_out = head_attention(positions[0], choice, rows, tail, head_weight, loc)

    with jax.named_scope("out"):
        gathered = lax.all_to_all(head_out, "seq", split_axis=0, concat_axis=0, tiled=True)
        gathered = gathered.reshape(E, -1)
        output = lax.dot_general(
            gathered, project_out, (((0,), (0,)), ((), ())), preferred_element_type=jnp.float32
        ).astype(jnp.bfloat16)
    return output[None]


def solution(mesh):
    in_specs = (
        P("enc", "seq", None, None, None),
        P("enc", None),
        P(),
        P(),
        P(),
        P("enc", None),
        P("enc", "seq", None),
        P(None, "seq"),
        P(),
        P(),
    )
    out_specs = P("enc", "seq", None)
    return jax.shard_map(shards, mesh=mesh, in_specs=in_specs, out_specs=out_specs, check_vma=False)
```

```python
import math
from functools import partial

import jax
import jax.numpy as jnp
from jax import lax
from jax.experimental import pallas as pl
from jax.experimental.pallas import tpu as pltpu
from jax.sharding import PartitionSpec as P

E = 768
HEADS = 16
WIDTH = E // HEADS
SEGMENT = 512
STEP_ROWS = 1024
SCALE = WIDTH**-0.5 * math.log2(math.e)


def attend(rate, offset, table, out_ref):
    length = table.shape[1]
    loc = out_ref.shape[2]
    spread = None
    if rate > 1:
        source = lax.broadcasted_iota(jnp.int32, (128, 128 * rate), 0)
        target = lax.broadcasted_iota(jnp.int32, (128, 128 * rate), 1)
        spread = (target == offset + rate * source).astype(jnp.float32).astype(jnp.bfloat16)
    lane = lax.broadcasted_iota(jnp.int32, (SEGMENT, 128), 1)
    def load(index):
        start = index * (SEGMENT * rate) + offset
        if rate == 1:
            rows = pl.ds(pl.multiple_of(index * SEGMENT, SEGMENT), SEGMENT)
        else:
            rows = pl.ds(start, SEGMENT, stride=rate)
        query_value = table[0, rows, :]
        keys = table[1, rows, :].astype(jnp.bfloat16)
        with_ones = jnp.where(lane == 112, 1.0, query_value).astype(jnp.bfloat16)
        return query_value.astype(jnp.bfloat16), keys, with_ones

    def score(loaded, part):
        queries, keys, _ = loaded
        return lax.dot_general(
            keys,
            queries[part * 512 : (part + 1) * 512],
            (((1,), (1,)), ((), ())),
            preferred_element_type=jnp.float32,
        )

    def finish(index, part, loaded, scores):
        top = jnp.max(scores, axis=0, keepdims=True)
        raised = jnp.exp2((scores - top) * SCALE).astype(jnp.bfloat16)
        mixed = lax.dot_general(
            loaded[2], raised, (((0,), (0,)), ((), ())), preferred_element_type=jnp.float32
        )
        result = (mixed[64:112] / mixed[112:113]).astype(jnp.bfloat16)
        if rate == 1:
            for block in range(512 // loc):
                out_ref[index * (SEGMENT // loc) + part * (512 // loc) + block] = result[
                    :, block * loc : (block + 1) * loc
                ]
            return
        blocks = 128 * rate // loc
        for piece in range(512 // 128):
            wide = jnp.dot(
                result[:, piece * 128 : (piece + 1) * 128],
                spread,
                preferred_element_type=jnp.float32,
            ).astype(jnp.bfloat16)
            first = (index * 4 + part * (512 // 128) + piece) * blocks
            for block in range(blocks):
                out_ref[first + block] = wide[:, block * loc : (block + 1) * loc]

    segments = length // (SEGMENT * rate)
    together = min(segments, 4)

    def group(step, carry):
        work = []
        for inner in range(together):
            index = step * together + inner
            loaded = load(index)
            work += [(index, part, loaded) for part in range(SEGMENT // 512)]
        ahead = [score(loaded, part) for _, part, loaded in work[:1]]
        for number, (index, part, loaded) in enumerate(work):
            if number + 1 < len(work):
                _, next_part, next_loaded = work[number + 1]
                ahead.append(score(next_loaded, next_part))
            finish(index, part, loaded, ahead[number])
        return carry

    lax.fori_loop(0, segments // together, group, 0)


def head_kernel(
    places, choice, rows_ref, fresh_ref, weight_ref, out_ref, table, fresh, held, arrived
):
    chunks = held.shape[0]

    def arrival(chunk):
        first = pl.multiple_of(chunk * STEP_ROWS, STEP_ROWS)
        return pltpu.make_async_copy(
            rows_ref.at[pl.ds(first, STEP_ROWS)], held.at[chunk], arrived.at[chunk]
        )

    for chunk in range(chunks):
        arrival(chunk).start()
    made_fresh = jnp.dot(fresh_ref[...], weight_ref[...], preferred_element_type=jnp.float32)
    made_fresh = made_fresh.astype(jnp.bfloat16).astype(jnp.float32)
    fresh[0] = made_fresh[:, :128]
    fresh[1] = made_fresh[:, 128:]

    def project(chunk, carry):
        arrival(chunk).wait()
        made = jnp.dot(held[chunk], weight_ref[...], preferred_element_type=jnp.float32)
        made = made.astype(jnp.bfloat16).astype(jnp.float32)
        block = pl.ds(pl.multiple_of(chunk * STEP_ROWS, STEP_ROWS), STEP_ROWS)
        table[0, block, :] = made[:, :128]
        table[1, block, :] = made[:, 128:]
        return carry

    lax.fori_loop(0, chunks, project, 0)

    def place(group, carry):
        for inner in range(8):
            tile = group * 8 + inner
            where = places[tile]
            for side in range(2):
                table[side, pl.ds(where, 1), :] = fresh[side, pl.ds(tile, 1), :]
        return carry

    lax.fori_loop(0, fresh.shape[1] // 8, place, 0)
    for rate in (1, 2, 4, 8):
        pl.when(choice[0] == rate)(partial(attend, rate, choice[1], table, out_ref))


def head_attention(places, choice, rows, fresh, weight, seq_count):
    length = rows.shape[0]
    loc = length // seq_count
    chunks = length // STEP_ROWS
    return pl.pallas_call(
        head_kernel,
        out_shape=jax.ShapeDtypeStruct((seq_count, WIDTH, loc), jnp.bfloat16),
        in_specs=[
            pl.BlockSpec(memory_space=pltpu.SMEM),
            pl.BlockSpec(memory_space=pltpu.SMEM),
            pl.BlockSpec(memory_space=pltpu.HBM),
            pl.BlockSpec(memory_space=pltpu.VMEM),
            pl.BlockSpec(memory_space=pltpu.VMEM),
        ],
        out_specs=pl.BlockSpec(memory_space=pltpu.VMEM),
        scratch_shapes=[
            pltpu.VMEM((2, length, 128), jnp.float32),
            pltpu.VMEM((2, fresh.shape[0], 128), jnp.float32),
            pltpu.VMEM((chunks, STEP_ROWS, E), jnp.bfloat16),
            pltpu.SemaphoreType.DMA((chunks,)),
        ],
        compiler_params=pltpu.CompilerParams(vmem_limit_bytes=48 * 1024 * 1024),
        cost_estimate=pl.CostEstimate(
            flops=2 * length * E * 256, bytes_accessed=0, transcendentals=0
        ),
    )(places, choice, rows, fresh, weight)


def regroup_kernel(shard, core, columns_ref, own_ref, other_ref):
    columns = columns_ref[...]
    count = columns.shape[1] // shard
    even, odd = (
        jnp.concatenate(
            [columns[:, j * shard : (j + 1) * shard] for j in range(first, count, 2)], axis=1
        )
        for first in range(2)
    )

    @pl.when(core[0] == 0)
    def _():
        own_ref[...] = even
        other_ref[...] = odd

    @pl.when(core[0] == 1)
    def _():
        own_ref[...] = odd
        other_ref[...] = even


def regroup(core, columns, shard):
    rows, depth = columns.shape
    half = jax.ShapeDtypeStruct((rows, depth // 2), columns.dtype)
    block = 128
    return pl.pallas_call(
        partial(regroup_kernel, shard),
        out_shape=(half, half),
        grid_spec=pltpu.PrefetchScalarGridSpec(
            num_scalar_prefetch=1,
            grid=(rows // block,),
            in_specs=[pl.BlockSpec((block, depth), lambda i, *_: (i, 0))],
            out_specs=[pl.BlockSpec((block, depth // 2), lambda i, *_: (i, 0))] * 2,
        ),
        compiler_params=pltpu.CompilerParams(vmem_limit_bytes=24 * 1024 * 1024),
        cost_estimate=pl.CostEstimate(
            flops=0, bytes_accessed=columns.size * 4, transcendentals=0
        ),
    )(core, columns)


def spread_to(shard, axis, count, groups=None):
    copies = jnp.broadcast_to(shard[None], (count,) + shard.shape)
    return lax.all_to_all(
        copies, axis, split_axis=0, concat_axis=0, tiled=True, axis_index_groups=groups
    )


def convolve(conv_weight, columns, ready):
    enc_count = lax.axis_size("enc")
    chips = enc_count // 2
    shard, channels = conv_weight.shape
    groups = [[2 * chip + core for chip in range(chips)] for core in range(2)]
    own = spread_to(conv_weight, "enc", chips, groups)
    core = (lax.axis_index("enc") % 2).astype(jnp.int32).reshape(1)
    own_columns, other_columns = regroup(core, columns, shard)
    own, own_columns, other_columns, ready = lax.optimization_barrier(
        (own, own_columns, other_columns, ready)
    )
    other = lax.ppermute(own, "enc", [(e, e ^ 1) for e in range(enc_count)])
    first = jnp.dot(
        own_columns, own.reshape(-1, channels), preferred_element_type=jnp.float32
    )
    second = jnp.dot(
        other_columns, other.reshape(-1, channels), preferred_element_type=jnp.float32
    )
    return first + second, ready


def shards(
    tile_maps,
    conv_weight,
    norm_gain,
    norm_bias,
    tile_proj,
    positions,
    slide_cache,
    project_in,
    project_out,
    head_rates,
):
    tile_count = tile_maps.shape[1]
    side_len = tile_maps.shape[2]
    channels = tile_maps.shape[4]
    seq_count = lax.axis_size("seq")
    my_index = lax.axis_index("seq")

    with jax.named_scope("rows"):
        rows = lax.all_gather(slide_cache[0], "seq", axis=0, tiled=True)

    with jax.named_scope("choice"):
        gap = jnp.zeros((E, 16), jnp.bfloat16)
        end = jnp.zeros((E, 80), jnp.bfloat16)
        queries, keys, values = jnp.split(project_in, 3, axis=1)
        head_weight = jnp.concatenate([queries, gap, values, gap, keys, end], axis=1)
        rate = head_rates[my_index]
        choice = jnp.stack([rate, my_index % rate]).astype(jnp.int32)

    with jax.named_scope("encode"):
        images = tile_maps[0]
        padded = jnp.pad(images, ((0, 0), (1, 1), (1, 1), (0, 0)))
        columns = jnp.concatenate(
            [
                padded[:, row_shift : row_shift + side_len, col_shift : col_shift + side_len, :]
                for row_shift in range(3)
                for col_shift in range(3)
            ],
            axis=-1,
        )
        columns = columns.reshape(tile_count * side_len * side_len, 9 * channels)
        convolved, (head_weight, choice) = convolve(conv_weight, columns, (head_weight, choice))
        activated = jnp.maximum(convolved * norm_gain + norm_bias, 0.0) + images.reshape(
            -1, channels
        ).astype(jnp.float32)
        pooled = jnp.mean(
            activated.reshape(tile_count, side_len * side_len, channels), axis=1
        ).astype(jnp.bfloat16)
    with jax.named_scope("fresh"):
        pooled = lax.all_gather(pooled, "seq", axis=0, tiled=True)
        fresh = jnp.dot(pooled, tile_proj, preferred_element_type=jnp.float32).astype(jnp.bfloat16)

    with jax.named_scope("head"):
        head_out = head_attention(positions[0], choice, rows, fresh, head_weight, seq_count)

    with jax.named_scope("out"):
        gathered = lax.all_to_all(head_out, "seq", split_axis=0, concat_axis=0, tiled=True)
        gathered = gathered.reshape(E, -1)
        output = lax.dot_general(
            gathered, project_out, (((0,), (0,)), ((), ())), preferred_element_type=jnp.float32
        ).astype(jnp.bfloat16)
    return output[None]


def solution(mesh):
    in_specs = (
        P("enc", "seq", None, None, None),
        P("enc", None),
        P(),
        P(),
        P(),
        P("enc", None),
        P("enc", "seq", None),
        P(None, "seq"),
        P(),
        P(),
    )
    out_specs = P("enc", "seq", None)
    return jax.shard_map(shards, mesh=mesh, in_specs=in_specs, out_specs=out_specs, check_vma=False)
```

```python
import math
from functools import partial

import jax
import jax.numpy as jnp
from jax import lax
from jax.experimental import pallas as pl
from jax.experimental.pallas import tpu as pltpu
from jax.sharding import PartitionSpec as P

E = 768
HEADS = 16
WIDTH = E // HEADS
SEGMENT = 512
STEP_ROWS = 1024
SCALE = WIDTH**-0.5 * math.log2(math.e)


def attend(rate, offset, table, out_ref):
    length = table.shape[1]
    loc = out_ref.shape[2]
    spread = None
    if rate > 1:
        source = lax.broadcasted_iota(jnp.int32, (128, 128 * rate), 0)
        target = lax.broadcasted_iota(jnp.int32, (128, 128 * rate), 1)
        spread = (target == offset + rate * source).astype(jnp.float32).astype(jnp.bfloat16)
    lane = lax.broadcasted_iota(jnp.int32, (SEGMENT, 128), 1)
    def load(index):
        start = index * (SEGMENT * rate) + offset
        if rate == 1:
            rows = pl.ds(pl.multiple_of(index * SEGMENT, SEGMENT), SEGMENT)
        else:
            rows = pl.ds(start, SEGMENT, stride=rate)
        query_value = table[0, rows, :]
        keys = table[1, rows, :].astype(jnp.bfloat16)
        with_ones = jnp.where(lane == 112, 1.0, query_value).astype(jnp.bfloat16)
        return query_value.astype(jnp.bfloat16), keys, with_ones

    def score(loaded, part):
        queries, keys, _ = loaded
        return lax.dot_general(
            keys,
            queries[part * 256 : (part + 1) * 256],
            (((1,), (1,)), ((), ())),
            preferred_element_type=jnp.float32,
        )

    def finish(index, part, loaded, scores):
        top = jnp.max(scores, axis=0, keepdims=True)
        raised = jnp.exp2((scores - top) * SCALE).astype(jnp.bfloat16)
        mixed = lax.dot_general(
            loaded[2], raised, (((0,), (0,)), ((), ())), preferred_element_type=jnp.float32
        )
        result = (mixed[64:112] / mixed[112:113]).astype(jnp.bfloat16)
        if rate == 1:
            for block in range(256 // loc):
                out_ref[index * (SEGMENT // loc) + part * (256 // loc) + block] = result[
                    :, block * loc : (block + 1) * loc
                ]
            return
        blocks = 128 * rate // loc
        for piece in range(256 // 128):
            wide = jnp.dot(
                result[:, piece * 128 : (piece + 1) * 128],
                spread,
                preferred_element_type=jnp.float32,
            ).astype(jnp.bfloat16)
            first = (index * 4 + part * (256 // 128) + piece) * blocks
            for block in range(blocks):
                out_ref[first + block] = wide[:, block * loc : (block + 1) * loc]

    segments = length // (SEGMENT * rate)
    together = min(segments, 8)

    def group(step, carry):
        work = []
        for inner in range(together):
            index = step * together + inner
            loaded = load(index)
            work += [(index, part, loaded) for part in range(SEGMENT // 256)]
        ahead = [score(loaded, part) for _, part, loaded in work[:3]]
        for number, (index, part, loaded) in enumerate(work):
            if number + 3 < len(work):
                _, next_part, next_loaded = work[number + 3]
                ahead.append(score(next_loaded, next_part))
            finish(index, part, loaded, ahead[number])
        return carry

    lax.fori_loop(0, segments // together, group, 0)


def head_kernel(
    places, choice, rows_ref, fresh_ref, weight_ref, out_ref, table, fresh, held, arrived
):
    chunks = held.shape[0]

    def arrival(chunk):
        first = pl.multiple_of(chunk * STEP_ROWS, STEP_ROWS)
        return pltpu.make_async_copy(
            rows_ref.at[pl.ds(first, STEP_ROWS)], held.at[chunk], arrived.at[chunk]
        )

    for chunk in range(chunks):
        arrival(chunk).start()
    made_fresh = jnp.dot(fresh_ref[...], weight_ref[...], preferred_element_type=jnp.float32)
    made_fresh = made_fresh.astype(jnp.bfloat16).astype(jnp.float32)
    fresh[0] = made_fresh[:, :128]
    fresh[1] = made_fresh[:, 128:]

    def project(chunk, carry):
        arrival(chunk).wait()
        made = jnp.dot(held[chunk], weight_ref[...], preferred_element_type=jnp.float32)
        made = made.astype(jnp.bfloat16).astype(jnp.float32)
        block = pl.ds(pl.multiple_of(chunk * STEP_ROWS, STEP_ROWS), STEP_ROWS)
        table[0, block, :] = made[:, :128]
        table[1, block, :] = made[:, 128:]
        return carry

    lax.fori_loop(0, chunks, project, 0)

    def place(group, carry):
        for inner in range(8):
            tile = group * 8 + inner
            where = places[tile]
            for side in range(2):
                table[side, pl.ds(where, 1), :] = fresh[side, pl.ds(tile, 1), :]
        return carry

    lax.fori_loop(0, fresh.shape[1] // 8, place, 0)
    for rate in (1, 2, 4, 8):
        pl.when(choice[0] == rate)(partial(attend, rate, choice[1], table, out_ref))


def head_attention(places, choice, rows, fresh, weight, seq_count):
    length = rows.shape[0]
    loc = length // seq_count
    chunks = length // STEP_ROWS
    return pl.pallas_call(
        head_kernel,
        out_shape=jax.ShapeDtypeStruct((seq_count, WIDTH, loc), jnp.bfloat16),
        in_specs=[
            pl.BlockSpec(memory_space=pltpu.SMEM),
            pl.BlockSpec(memory_space=pltpu.SMEM),
            pl.BlockSpec(memory_space=pltpu.HBM),
            pl.BlockSpec(memory_space=pltpu.VMEM),
            pl.BlockSpec(memory_space=pltpu.VMEM),
        ],
        out_specs=pl.BlockSpec(memory_space=pltpu.VMEM),
        scratch_shapes=[
            pltpu.VMEM((2, length, 128), jnp.float32),
            pltpu.VMEM((2, fresh.shape[0], 128), jnp.float32),
            pltpu.VMEM((chunks, STEP_ROWS, E), jnp.bfloat16),
            pltpu.SemaphoreType.DMA((chunks,)),
        ],
        compiler_params=pltpu.CompilerParams(vmem_limit_bytes=48 * 1024 * 1024),
        cost_estimate=pl.CostEstimate(
            flops=2 * length * E * 256, bytes_accessed=0, transcendentals=0
        ),
    )(places, choice, rows, fresh, weight)


def regroup_kernel(shard, core, columns_ref, own_ref, other_ref):
    columns = columns_ref[...]
    count = columns.shape[1] // shard
    even, odd = (
        jnp.concatenate(
            [columns[:, j * shard : (j + 1) * shard] for j in range(first, count, 2)], axis=1
        )
        for first in range(2)
    )

    @pl.when(core[0] == 0)
    def _():
        own_ref[...] = even
        other_ref[...] = odd

    @pl.when(core[0] == 1)
    def _():
        own_ref[...] = odd
        other_ref[...] = even


def regroup(core, columns, shard):
    rows, depth = columns.shape
    half = jax.ShapeDtypeStruct((rows, depth // 2), columns.dtype)
    block = 128
    return pl.pallas_call(
        partial(regroup_kernel, shard),
        out_shape=(half, half),
        grid_spec=pltpu.PrefetchScalarGridSpec(
            num_scalar_prefetch=1,
            grid=(rows // block,),
            in_specs=[pl.BlockSpec((block, depth), lambda i, *_: (i, 0))],
            out_specs=[pl.BlockSpec((block, depth // 2), lambda i, *_: (i, 0))] * 2,
        ),
        compiler_params=pltpu.CompilerParams(vmem_limit_bytes=24 * 1024 * 1024),
        cost_estimate=pl.CostEstimate(
            flops=0, bytes_accessed=columns.size * 4, transcendentals=0
        ),
    )(core, columns)


def spread_to(shard, axis, count, groups=None):
    copies = jnp.broadcast_to(shard[None], (count,) + shard.shape)
    return lax.all_to_all(
        copies, axis, split_axis=0, concat_axis=0, tiled=True, axis_index_groups=groups
    )


def convolve(conv_weight, columns, ready):
    enc_count = lax.axis_size("enc")
    chips = enc_count // 2
    shard, channels = conv_weight.shape
    groups = [[2 * chip + core for chip in range(chips)] for core in range(2)]
    own = spread_to(conv_weight, "enc", chips, groups)
    core = (lax.axis_index("enc") % 2).astype(jnp.int32).reshape(1)
    own_columns, other_columns = regroup(core, columns, shard)
    own, own_columns, other_columns, ready = lax.optimization_barrier(
        (own, own_columns, other_columns, ready)
    )
    other = lax.ppermute(own, "enc", [(e, e ^ 1) for e in range(enc_count)])
    first = jnp.dot(
        own_columns, own.reshape(-1, channels), preferred_element_type=jnp.float32
    )
    second = jnp.dot(
        other_columns, other.reshape(-1, channels), preferred_element_type=jnp.float32
    )
    return first + second, ready


def shards(
    tile_maps,
    conv_weight,
    norm_gain,
    norm_bias,
    tile_proj,
    positions,
    slide_cache,
    project_in,
    project_out,
    head_rates,
):
    tile_count = tile_maps.shape[1]
    side_len = tile_maps.shape[2]
    channels = tile_maps.shape[4]
    seq_count = lax.axis_size("seq")
    my_index = lax.axis_index("seq")

    with jax.named_scope("rows"):
        rows = lax.all_gather(slide_cache[0], "seq", axis=0, tiled=True)

    with jax.named_scope("choice"):
        gap = jnp.zeros((E, 16), jnp.bfloat16)
        end = jnp.zeros((E, 80), jnp.bfloat16)
        queries, keys, values = jnp.split(project_in, 3, axis=1)
        head_weight = jnp.concatenate([queries, gap, values, gap, keys, end], axis=1)
        rate = head_rates[my_index]
        choice = jnp.stack([rate, my_index % rate]).astype(jnp.int32)

    with jax.named_scope("encode"):
        images = tile_maps[0]
        padded = jnp.pad(images, ((0, 0), (1, 1), (1, 1), (0, 0)))
        columns = jnp.concatenate(
            [
                padded[:, row_shift : row_shift + side_len, col_shift : col_shift + side_len, :]
                for row_shift in range(3)
                for col_shift in range(3)
            ],
            axis=-1,
        )
        columns = columns.reshape(tile_count * side_len * side_len, 9 * channels)
        convolved, (head_weight, choice) = convolve(conv_weight, columns, (head_weight, choice))
        activated = jnp.maximum(convolved * norm_gain + norm_bias, 0.0) + images.reshape(
            -1, channels
        ).astype(jnp.float32)
        pooled = jnp.mean(
            activated.reshape(tile_count, side_len * side_len, channels), axis=1
        ).astype(jnp.bfloat16)
    with jax.named_scope("fresh"):
        pooled = lax.all_gather(pooled, "seq", axis=0, tiled=True)
        fresh = jnp.dot(pooled, tile_proj, preferred_element_type=jnp.float32).astype(jnp.bfloat16)

    with jax.named_scope("head"):
        head_out = head_attention(positions[0], choice, rows, fresh, head_weight, seq_count)

    with jax.named_scope("out"):
        gathered = lax.all_to_all(head_out, "seq", split_axis=0, concat_axis=0, tiled=True)
        gathered = gathered.reshape(E, -1)
        output = lax.dot_general(
            gathered, project_out, (((0,), (0,)), ((), ())), preferred_element_type=jnp.float32
        ).astype(jnp.bfloat16)
    return output[None]


def solution(mesh):
    in_specs = (
        P("enc", "seq", None, None, None),
        P("enc", None),
        P(),
        P(),
        P(),
        P("enc", None),
        P("enc", "seq", None),
        P(None, "seq"),
        P(),
        P(),
    )
    out_specs = P("enc", "seq", None)
    return jax.shard_map(shards, mesh=mesh, in_specs=in_specs, out_specs=out_specs, check_vma=False)
```

```python
import math
from functools import partial

import jax
import jax.numpy as jnp
from jax import lax
from jax.experimental import pallas as pl
from jax.experimental.pallas import tpu as pltpu
from jax.sharding import PartitionSpec as P

E = 768
HEADS = 16
WIDTH = E // HEADS
SEGMENT = 512
STEP_ROWS = 1024
SPARE = 8
SCALE = WIDTH**-0.5 * math.log2(math.e)


def attend(rate, offset, table, out_ref):
    length = table.shape[1] - SPARE
    loc = out_ref.shape[2]
    spread = None
    if rate > 1:
        source = lax.broadcasted_iota(jnp.int32, (128, 128 * rate), 0)
        target = lax.broadcasted_iota(jnp.int32, (128, 128 * rate), 1)
        spread = (target == offset + rate * source).astype(jnp.float32).astype(jnp.bfloat16)
    lane = lax.broadcasted_iota(jnp.int32, (SEGMENT, 128), 1)
    def load(index):
        start = index * (SEGMENT * rate) + offset
        if rate == 1:
            rows = pl.ds(pl.multiple_of(index * SEGMENT, SEGMENT), SEGMENT)
        else:
            rows = pl.ds(start, SEGMENT, stride=rate)
        query_value = table[0, rows, :]
        keys = table[1, rows, :].astype(jnp.bfloat16)
        with_ones = jnp.where(lane == 112, 1.0, query_value).astype(jnp.bfloat16)
        return query_value.astype(jnp.bfloat16), keys, with_ones

    def score(loaded, part):
        queries, keys, _ = loaded
        return lax.dot_general(
            keys,
            queries[part * 256 : (part + 1) * 256],
            (((1,), (1,)), ((), ())),
            preferred_element_type=jnp.float32,
        )

    def finish(index, part, loaded, scores):
        top = jnp.max(scores, axis=0, keepdims=True)
        raised = jnp.exp2((scores - top) * SCALE).astype(jnp.bfloat16)
        mixed = lax.dot_general(
            loaded[2], raised, (((0,), (0,)), ((), ())), preferred_element_type=jnp.float32
        )
        result = (mixed[64:112] / mixed[112:113]).astype(jnp.bfloat16)
        if rate == 1:
            for block in range(256 // loc):
                out_ref[index * (SEGMENT // loc) + part * (256 // loc) + block] = result[
                    :, block * loc : (block + 1) * loc
                ]
            return
        blocks = 128 * rate // loc
        for piece in range(256 // 128):
            wide = jnp.dot(
                result[:, piece * 128 : (piece + 1) * 128],
                spread,
                preferred_element_type=jnp.float32,
            ).astype(jnp.bfloat16)
            first = (index * 4 + part * (256 // 128) + piece) * blocks
            for block in range(blocks):
                out_ref[first + block] = wide[:, block * loc : (block + 1) * loc]

    segments = length // (SEGMENT * rate)
    together = min(segments, 8)

    def group(step, carry):
        work = []
        for inner in range(together):
            index = step * together + inner
            loaded = load(index)
            work += [(index, part, loaded) for part in range(SEGMENT // 256)]
        ahead = [score(loaded, part) for _, part, loaded in work[:3]]
        for number, (index, part, loaded) in enumerate(work):
            if number + 3 < len(work):
                _, next_part, next_loaded = work[number + 3]
                ahead.append(score(next_loaded, next_part))
            finish(index, part, loaded, ahead[number])
        return carry

    lax.fori_loop(0, segments // together, group, 0)


def head_kernel(
    places, choice, rows_ref, fresh_ref, weight_ref, out_ref, table, fresh, held, arrived
):
    chunks = held.shape[0]

    def arrival(chunk):
        first = pl.multiple_of(chunk * STEP_ROWS, STEP_ROWS)
        return pltpu.make_async_copy(
            rows_ref.at[pl.ds(first, STEP_ROWS)], held.at[chunk], arrived.at[chunk]
        )

    for chunk in range(chunks):
        arrival(chunk).start()
    made_fresh = jnp.dot(fresh_ref[...], weight_ref[...], preferred_element_type=jnp.float32)
    made_fresh = made_fresh.astype(jnp.bfloat16).astype(jnp.float32)
    fresh[0] = made_fresh[:, :128]
    fresh[1] = made_fresh[:, 128:]

    def project(chunk, carry):
        arrival(chunk).wait()
        made = jnp.dot(held[chunk], weight_ref[...], preferred_element_type=jnp.float32)
        made = made.astype(jnp.bfloat16).astype(jnp.float32)
        block = pl.ds(pl.multiple_of(chunk * STEP_ROWS, STEP_ROWS), STEP_ROWS)
        table[0, block, :] = made[:, :128]
        table[1, block, :] = made[:, 128:]
        return carry

    lax.fori_loop(0, chunks, project, 0)

    def place(group, carry):
        for inner in range(8):
            tile = group * 8 + inner
            where = places[tile]
            for side in range(2):
                table[side, pl.ds(where, 1), :] = fresh[side, pl.ds(tile, 1), :]
        return carry

    lax.fori_loop(0, fresh.shape[1] // 8, place, 0)
    for rate in (1, 2, 4, 8):
        pl.when(choice[0] == rate)(partial(attend, rate, choice[1], table, out_ref))


def head_attention(places, choice, rows, fresh, weight, seq_count):
    length = rows.shape[0]
    loc = length // seq_count
    chunks = length // STEP_ROWS
    return pl.pallas_call(
        head_kernel,
        out_shape=jax.ShapeDtypeStruct((seq_count, WIDTH, loc), jnp.bfloat16),
        in_specs=[
            pl.BlockSpec(memory_space=pltpu.SMEM),
            pl.BlockSpec(memory_space=pltpu.SMEM),
            pl.BlockSpec(memory_space=pltpu.HBM),
            pl.BlockSpec(memory_space=pltpu.VMEM),
            pl.BlockSpec(memory_space=pltpu.VMEM),
        ],
        out_specs=pl.BlockSpec(memory_space=pltpu.VMEM),
        scratch_shapes=[
            pltpu.VMEM((2, length + SPARE, 128), jnp.float32),
            pltpu.VMEM((2, fresh.shape[0], 128), jnp.float32),
            pltpu.VMEM((chunks, STEP_ROWS, E), jnp.bfloat16),
            pltpu.SemaphoreType.DMA((chunks,)),
        ],
        compiler_params=pltpu.CompilerParams(vmem_limit_bytes=48 * 1024 * 1024),
        cost_estimate=pl.CostEstimate(
            flops=2 * length * E * 256, bytes_accessed=0, transcendentals=0
        ),
    )(places, choice, rows, fresh, weight)


def regroup_kernel(shard, core, columns_ref, own_ref, other_ref):
    columns = columns_ref[...]
    count = columns.shape[1] // shard
    even, odd = (
        jnp.concatenate(
            [columns[:, j * shard : (j + 1) * shard] for j in range(first, count, 2)], axis=1
        )
        for first in range(2)
    )

    @pl.when(core[0] == 0)
    def _():
        own_ref[...] = even
        other_ref[...] = odd

    @pl.when(core[0] == 1)
    def _():
        own_ref[...] = odd
        other_ref[...] = even


def regroup(core, columns, shard):
    rows, depth = columns.shape
    half = jax.ShapeDtypeStruct((rows, depth // 2), columns.dtype)
    block = 128
    return pl.pallas_call(
        partial(regroup_kernel, shard),
        out_shape=(half, half),
        grid_spec=pltpu.PrefetchScalarGridSpec(
            num_scalar_prefetch=1,
            grid=(rows // block,),
            in_specs=[pl.BlockSpec((block, depth), lambda i, *_: (i, 0))],
            out_specs=[pl.BlockSpec((block, depth // 2), lambda i, *_: (i, 0))] * 2,
        ),
        compiler_params=pltpu.CompilerParams(vmem_limit_bytes=24 * 1024 * 1024),
        cost_estimate=pl.CostEstimate(
            flops=0, bytes_accessed=columns.size * 4, transcendentals=0
        ),
    )(core, columns)


def spread_to(shard, axis, count, groups=None):
    copies = jnp.broadcast_to(shard[None], (count,) + shard.shape)
    return lax.all_to_all(
        copies, axis, split_axis=0, concat_axis=0, tiled=True, axis_index_groups=groups
    )


def convolve(conv_weight, columns, ready):
    enc_count = lax.axis_size("enc")
    chips = enc_count // 2
    shard, channels = conv_weight.shape
    groups = [[2 * chip + core for chip in range(chips)] for core in range(2)]
    own = spread_to(conv_weight, "enc", chips, groups)
    core = (lax.axis_index("enc") % 2).astype(jnp.int32).reshape(1)
    own_columns, other_columns = regroup(core, columns, shard)
    own, own_columns, other_columns, ready = lax.optimization_barrier(
        (own, own_columns, other_columns, ready)
    )
    other = lax.ppermute(own, "enc", [(e, e ^ 1) for e in range(enc_count)])
    first = jnp.dot(
        own_columns, own.reshape(-1, channels), preferred_element_type=jnp.float32
    )
    second = jnp.dot(
        other_columns, other.reshape(-1, channels), preferred_element_type=jnp.float32
    )
    return first + second, ready


def shards(
    tile_maps,
    conv_weight,
    norm_gain,
    norm_bias,
    tile_proj,
    positions,
    slide_cache,
    project_in,
    project_out,
    head_rates,
):
    tile_count = tile_maps.shape[1]
    side_len = tile_maps.shape[2]
    channels = tile_maps.shape[4]
    seq_count = lax.axis_size("seq")
    my_index = lax.axis_index("seq")

    with jax.named_scope("rows"):
        rows = lax.all_gather(slide_cache[0], "seq", axis=0, tiled=True)

    with jax.named_scope("choice"):
        gap = jnp.zeros((E, 16), jnp.bfloat16)
        end = jnp.zeros((E, 80), jnp.bfloat16)
        queries, keys, values = jnp.split(project_in, 3, axis=1)
        head_weight = jnp.concatenate([queries, gap, values, gap, keys, end], axis=1)
        rate = head_rates[my_index]
        choice = jnp.stack([rate, my_index % rate]).astype(jnp.int32)

    with jax.named_scope("encode"):
        images = tile_maps[0]
        padded = jnp.pad(images, ((0, 0), (1, 1), (1, 1), (0, 0)))
        columns = jnp.concatenate(
            [
                padded[:, row_shift : row_shift + side_len, col_shift : col_shift + side_len, :]
                for row_shift in range(3)
                for col_shift in range(3)
            ],
            axis=-1,
        )
        columns = columns.reshape(tile_count * side_len * side_len, 9 * channels)
        convolved, (head_weight, choice) = convolve(conv_weight, columns, (head_weight, choice))
        activated = jnp.maximum(convolved * norm_gain + norm_bias, 0.0) + images.reshape(
            -1, channels
        ).astype(jnp.float32)
        pooled = jnp.mean(
            activated.reshape(tile_count, side_len * side_len, channels), axis=1
        ).astype(jnp.bfloat16)
    with jax.named_scope("fresh"):
        pooled = lax.all_gather(pooled, "seq", axis=0, tiled=True)
        fresh = jnp.dot(pooled, tile_proj, preferred_element_type=jnp.float32).astype(jnp.bfloat16)

    with jax.named_scope("head"):
        head_out = head_attention(positions[0], choice, rows, fresh, head_weight, seq_count)

    with jax.named_scope("out"):
        gathered = lax.all_to_all(head_out, "seq", split_axis=0, concat_axis=0, tiled=True)
        gathered = gathered.reshape(E, -1)
        output = lax.dot_general(
            gathered, project_out, (((0,), (0,)), ((), ())), preferred_element_type=jnp.float32
        ).astype(jnp.bfloat16)
    return output[None]


def solution(mesh):
    in_specs = (
        P("enc", "seq", None, None, None),
        P("enc", None),
        P(),
        P(),
        P(),
        P("enc", None),
        P("enc", "seq", None),
        P(None, "seq"),
        P(),
        P(),
    )
    out_specs = P("enc", "seq", None)
    return jax.shard_map(shards, mesh=mesh, in_specs=in_specs, out_specs=out_specs, check_vma=False)
```

```python
import math
from functools import partial

import jax
import jax.numpy as jnp
from jax import lax
from jax.experimental import pallas as pl
from jax.experimental.pallas import tpu as pltpu
from jax.sharding import PartitionSpec as P

E = 768
HEADS = 16
WIDTH = E // HEADS
SEGMENT = 512
STEP_ROWS = 1024
SPARE = 8
SCALE = WIDTH**-0.5 * math.log2(math.e)


def attend(rate, offset, table, out_ref):
    length = table.shape[1] - SPARE
    loc = out_ref.shape[2]
    spread = None
    if rate > 1:
        source = lax.broadcasted_iota(jnp.int32, (128, 128 * rate), 0)
        target = lax.broadcasted_iota(jnp.int32, (128, 128 * rate), 1)
        spread = (target == offset + rate * source).astype(jnp.float32).astype(jnp.bfloat16)
    lane = lax.broadcasted_iota(jnp.int32, (SEGMENT, 128), 1)
    def load(index):
        start = index * (SEGMENT * rate) + offset
        if rate == 1:
            rows = pl.ds(pl.multiple_of(index * SEGMENT, SEGMENT), SEGMENT)
        else:
            rows = pl.ds(start, SEGMENT, stride=rate)
        query_value = table[0, rows, :]
        keys = table[1, rows, :].astype(jnp.bfloat16)
        with_ones = jnp.where(lane == 112, 1.0, query_value).astype(jnp.bfloat16)
        return query_value.astype(jnp.bfloat16), keys, with_ones

    def score(loaded, part):
        queries, keys, _ = loaded
        return lax.dot_general(
            keys,
            queries[part * 256 : (part + 1) * 256],
            (((1,), (1,)), ((), ())),
            preferred_element_type=jnp.float32,
        )

    def finish(index, part, loaded, scores):
        top = jnp.max(scores, axis=0, keepdims=True)
        raised = jnp.exp2((scores - top) * SCALE).astype(jnp.bfloat16)
        mixed = lax.dot_general(
            loaded[2], raised, (((0,), (0,)), ((), ())), preferred_element_type=jnp.float32
        )
        result = (mixed[64:112] / mixed[112:113]).astype(jnp.bfloat16)
        if rate == 1:
            for block in range(256 // loc):
                out_ref[index * (SEGMENT // loc) + part * (256 // loc) + block] = result[
                    :, block * loc : (block + 1) * loc
                ]
            return
        blocks = 128 * rate // loc
        for piece in range(256 // 128):
            wide = jnp.dot(
                result[:, piece * 128 : (piece + 1) * 128],
                spread,
                preferred_element_type=jnp.float32,
            ).astype(jnp.bfloat16)
            first = (index * 4 + part * (256 // 128) + piece) * blocks
            for block in range(blocks):
                out_ref[first + block] = wide[:, block * loc : (block + 1) * loc]

    segments = length // (SEGMENT * rate)
    together = min(segments, 8)

    def group(step, carry):
        work = []
        for inner in range(together):
            index = step * together + inner
            loaded = load(index)
            work += [(index, part, loaded) for part in range(SEGMENT // 256)]
        ahead = [score(loaded, part) for _, part, loaded in work[:3]]
        for number, (index, part, loaded) in enumerate(work):
            if number + 3 < len(work):
                _, next_part, next_loaded = work[number + 3]
                ahead.append(score(next_loaded, next_part))
            finish(index, part, loaded, ahead[number])
        return carry

    lax.fori_loop(0, segments // together, group, 0)


def head_kernel(
    places, choice, rows_ref, fresh, weight_ref, out_ref, table, held, arrived
):
    chunks = held.shape[0]

    def arrival(chunk):
        first = pl.multiple_of(chunk * STEP_ROWS, STEP_ROWS)
        return pltpu.make_async_copy(
            rows_ref.at[pl.ds(first, STEP_ROWS)], held.at[chunk], arrived.at[chunk]
        )

    for chunk in range(chunks):
        arrival(chunk).start()

    def project(chunk, carry):
        arrival(chunk).wait()
        made = jnp.dot(held[chunk], weight_ref[...], preferred_element_type=jnp.float32)
        made = made.astype(jnp.bfloat16).astype(jnp.float32)
        block = pl.ds(pl.multiple_of(chunk * STEP_ROWS, STEP_ROWS), STEP_ROWS)
        table[0, block, :] = made[:, :128]
        table[1, block, :] = made[:, 128:]
        return carry

    lax.fori_loop(0, chunks, project, 0)

    def place(group, carry):
        for inner in range(8):
            tile = group * 8 + inner
            where = places[tile]
            for side in range(2):
                table[side, pl.ds(where, 1), :] = fresh[side, pl.ds(tile, 1), :]
        return carry

    lax.fori_loop(0, fresh.shape[1] // 8, place, 0)
    for rate in (1, 2, 4, 8):
        pl.when(choice[0] == rate)(partial(attend, rate, choice[1], table, out_ref))


def head_attention(places, choice, rows, fresh, weight, seq_count):
    length = rows.shape[0]
    loc = length // seq_count
    chunks = length // STEP_ROWS
    return pl.pallas_call(
        head_kernel,
        out_shape=jax.ShapeDtypeStruct((seq_count, WIDTH, loc), jnp.bfloat16),
        in_specs=[
            pl.BlockSpec(memory_space=pltpu.SMEM),
            pl.BlockSpec(memory_space=pltpu.SMEM),
            pl.BlockSpec(memory_space=pltpu.HBM),
            pl.BlockSpec(memory_space=pltpu.VMEM),
            pl.BlockSpec(memory_space=pltpu.VMEM),
        ],
        out_specs=pl.BlockSpec(memory_space=pltpu.VMEM),
        scratch_shapes=[
            pltpu.VMEM((2, length + SPARE, 128), jnp.float32),
            pltpu.VMEM((chunks, STEP_ROWS, E), jnp.bfloat16),
            pltpu.SemaphoreType.DMA((chunks,)),
        ],
        compiler_params=pltpu.CompilerParams(vmem_limit_bytes=48 * 1024 * 1024),
        cost_estimate=pl.CostEstimate(
            flops=2 * length * E * 256, bytes_accessed=0, transcendentals=0
        ),
    )(places, choice, rows, fresh, weight)


def regroup_kernel(shard, core, columns_ref, own_ref, other_ref):
    columns = columns_ref[...]
    count = columns.shape[1] // shard
    even, odd = (
        jnp.concatenate(
            [columns[:, j * shard : (j + 1) * shard] for j in range(first, count, 2)], axis=1
        )
        for first in range(2)
    )

    @pl.when(core[0] == 0)
    def _():
        own_ref[...] = even
        other_ref[...] = odd

    @pl.when(core[0] == 1)
    def _():
        own_ref[...] = odd
        other_ref[...] = even


def regroup(core, columns, shard):
    rows, depth = columns.shape
    half = jax.ShapeDtypeStruct((rows, depth // 2), columns.dtype)
    block = 128
    return pl.pallas_call(
        partial(regroup_kernel, shard),
        out_shape=(half, half),
        grid_spec=pltpu.PrefetchScalarGridSpec(
            num_scalar_prefetch=1,
            grid=(rows // block,),
            in_specs=[pl.BlockSpec((block, depth), lambda i, *_: (i, 0))],
            out_specs=[pl.BlockSpec((block, depth // 2), lambda i, *_: (i, 0))] * 2,
        ),
        compiler_params=pltpu.CompilerParams(vmem_limit_bytes=24 * 1024 * 1024),
        cost_estimate=pl.CostEstimate(
            flops=0, bytes_accessed=columns.size * 4, transcendentals=0
        ),
    )(core, columns)


def spread_to(shard, axis, count, groups=None):
    copies = jnp.broadcast_to(shard[None], (count,) + shard.shape)
    return lax.all_to_all(
        copies, axis, split_axis=0, concat_axis=0, tiled=True, axis_index_groups=groups
    )


def convolve(conv_weight, columns, ready):
    enc_count = lax.axis_size("enc")
    chips = enc_count // 2
    shard, channels = conv_weight.shape
    groups = [[2 * chip + core for chip in range(chips)] for core in range(2)]
    own = spread_to(conv_weight, "enc", chips, groups)
    core = (lax.axis_index("enc") % 2).astype(jnp.int32).reshape(1)
    own_columns, other_columns = regroup(core, columns, shard)
    own, own_columns, other_columns, ready = lax.optimization_barrier(
        (own, own_columns, other_columns, ready)
    )
    other = lax.ppermute(own, "enc", [(e, e ^ 1) for e in range(enc_count)])
    first = jnp.dot(
        own_columns, own.reshape(-1, channels), preferred_element_type=jnp.float32
    )
    second = jnp.dot(
        other_columns, other.reshape(-1, channels), preferred_element_type=jnp.float32
    )
    return first + second, ready


def shards(
    tile_maps,
    conv_weight,
    norm_gain,
    norm_bias,
    tile_proj,
    positions,
    slide_cache,
    project_in,
    project_out,
    head_rates,
):
    tile_count = tile_maps.shape[1]
    side_len = tile_maps.shape[2]
    channels = tile_maps.shape[4]
    seq_count = lax.axis_size("seq")
    my_index = lax.axis_index("seq")

    with jax.named_scope("rows"):
        rows = lax.all_gather(slide_cache[0], "seq", axis=0, tiled=True)

    with jax.named_scope("choice"):
        gap = jnp.zeros((E, 16), jnp.bfloat16)
        end = jnp.zeros((E, 80), jnp.bfloat16)
        queries, keys, values = jnp.split(project_in, 3, axis=1)
        head_weight = jnp.concatenate([queries, gap, values, gap, keys, end], axis=1)
        rate = head_rates[my_index]
        choice = jnp.stack([rate, my_index % rate]).astype(jnp.int32)

    with jax.named_scope("encode"):
        images = tile_maps[0]
        padded = jnp.pad(images, ((0, 0), (1, 1), (1, 1), (0, 0)))
        columns = jnp.concatenate(
            [
                padded[:, row_shift : row_shift + side_len, col_shift : col_shift + side_len, :]
                for row_shift in range(3)
                for col_shift in range(3)
            ],
            axis=-1,
        )
        columns = columns.reshape(tile_count * side_len * side_len, 9 * channels)
        convolved, (head_weight, choice) = convolve(conv_weight, columns, (head_weight, choice))
        activated = jnp.maximum(convolved * norm_gain + norm_bias, 0.0) + images.reshape(
            -1, channels
        ).astype(jnp.float32)
        pooled = jnp.mean(
            activated.reshape(tile_count, side_len * side_len, channels), axis=1
        ).astype(jnp.bfloat16)
    with jax.named_scope("fresh"):
        pooled = lax.all_gather(pooled, "seq", axis=0, tiled=True)
        fresh = jnp.dot(pooled, tile_proj, preferred_element_type=jnp.float32).astype(jnp.bfloat16)

    with jax.named_scope("head"):
        made = jnp.dot(fresh, head_weight, preferred_element_type=jnp.float32)
        made = made.astype(jnp.bfloat16).astype(jnp.float32)
        fresh = jnp.stack([made[:, :128], made[:, 128:]])
        head_out = head_attention(positions[0], choice, rows, fresh, head_weight, seq_count)

    with jax.named_scope("out"):
        gathered = lax.all_to_all(head_out, "seq", split_axis=0, concat_axis=0, tiled=True)
        gathered = gathered.reshape(E, -1)
        output = lax.dot_general(
            gathered, project_out, (((0,), (0,)), ((), ())), preferred_element_type=jnp.float32
        ).astype(jnp.bfloat16)
    return output[None]


def solution(mesh):
    in_specs = (
        P("enc", "seq", None, None, None),
        P("enc", None),
        P(),
        P(),
        P(),
        P("enc", None),
        P("enc", "seq", None),
        P(None, "seq"),
        P(),
        P(),
    )
    out_specs = P("enc", "seq", None)
    return jax.shard_map(shards, mesh=mesh, in_specs=in_specs, out_specs=out_specs, check_vma=False)
```
